256 devices in a mesh: width: 8 (over y, core), hidden: 32 (over x, z).
Axes of the slice: x: 4, y: 4, z: 8, core: 2. Of those that a mesh axis runs over, the one named last changes fastest.
Arguments:
- start_latent: float32 [512, 6144], P(None, 'width'), may hold values from -6 to 6
- target_one: float32 [512, 6144], P(None, 'width'), may hold values from -6 to 6
- target_two: float32 [512, 6144], P(None, 'width'), may hold values from -6 to 6
- w_up: bfloat16 [6144, 24576], P('width', 'hidden'), may hold values from -0.078125 to 0.078125
- w_down: bfloat16 [24576, 6144], P('hidden', 'width'), may hold values from -0.0390625 to 0.0390625
Outputs:
- grad_start: float32 [512, 6144], P('hidden', 'width')
- grad_up: float32 [6144, 24576], P('width', 'hidden')
- grad_down: float32 [24576, 6144], P('hidden', 'width')
The draws below stay inside these ranges and needn't reach their ends.
All inputs are finite; a program needn't handle non-finite values.
Results may differ from the reference program's by a relative error of at most 0.018.
Values may be sent and summed in bfloat16 or wider, within the bound.
No kernel may reach another device: no remote copies, remote signals or barrier semaphores. Data moves between devices by JAX's collectives and lax.ppermute only.
A program may use at most 64 MiB of HBM per device.

```python
import math
import jax
import jax.numpy as jnp
from jax import lax

D = 6144
FF = 24576
ROWS = 512
N_WIDTH = 8


def block_levels(key, shape, cuts, least, largest):
    def one(position, blocks):
        heights = jax.random.uniform(jax.random.fold_in(jax.random.fold_in(key, 6), position), (blocks,), jnp.float32, least / len(cuts), largest / len(cuts))
        return jnp.repeat(jnp.exp(heights), shape[position] // blocks).reshape((-1,) + (1,) * (len(shape) - position - 1))

    loudness = one(*cuts[0])
    for cut in cuts[1:]:
        loudness = loudness * one(*cut)
    return loudness


def noise(key, shape, width, reach, shards=(), kind=jnp.bfloat16):
    entries = width * jax.random.normal(key, shape, jnp.float32)
    if shards:
        entries = entries * block_levels(key, shape, shards, -0.22, 0.18)
    return jnp.clip(entries, -reach, reach).astype(kind)


def setup_inputs(seed: int = 0) -> dict:
    seeds = jax.random.split(jax.random.key(seed), 6)
    start_latent = noise(seeds[0], (ROWS, D), 1.0, 6.0, ((1, 8),), jnp.float32)
    target_one = noise(seeds[1], (ROWS, D), 1.0, 6.0, ((1, 8),), jnp.float32)
    target_two = noise(seeds[2], (ROWS, D), 1.0, 6.0, ((1, 8),), jnp.float32)
    w_up = noise(seeds[3], (D, FF), D ** -0.5, 0.078125, ((0, 8), (1, 32)))
    w_down = noise(seeds[4], (FF, D), FF ** -0.5, 0.0390625, ((0, 32), (1, 8)))
    return dict(start_latent=start_latent, target_one=target_one, target_two=target_two, w_up=w_up, w_down=w_down)


gelu_scale = math.sqrt(2.0 / math.pi)
cubic_coef = 0.044715

def gelu_parts(preact):
    inner = gelu_scale * (preact + cubic_coef * preact * preact * preact)
    tangent = jnp.tanh(inner)
    value_out = 0.5 * preact * (1.0 + tangent)
    slope_out = 0.5 * (1.0 + tangent) + 0.5 * preact * (1.0 - tangent * tangent) * gelu_scale * (1.0 + 3.0 * cubic_coef * preact * preact)
    return (value_out, slope_out)

def block_sum(left_mat, right_mat, right_rows):
    block_width = left_mat.shape[1] // N_WIDTH
    summed = jnp.zeros((left_mat.shape[0], right_mat.shape[1] if right_rows else right_mat.shape[0]), jnp.float32)

    def add_block(accum, block_index):
        first_col = (block_index * block_width).astype(jnp.int32)
        left_cols = lax.dynamic_slice_in_dim(left_mat, first_col, block_width, 1)
        if right_rows:
            right_part = lax.dynamic_slice_in_dim(right_mat, first_col, block_width, 0)
            product = jnp.dot(left_cols, right_part, preferred_element_type=jnp.float32)
        else:
            right_part = lax.dynamic_slice_in_dim(right_mat, first_col, block_width, 1)
            product = jnp.dot(left_cols, right_part.T, preferred_element_type=jnp.float32)
        rounded = lax.optimization_barrier(product.astype(jnp.bfloat16))
        return (accum + rounded.astype(jnp.float32), None)
    summed, unused = lax.scan(add_block, summed, jnp.arange(N_WIDTH, dtype=jnp.int32))
    return summed

def reference(start_latent, target_one, target_two, w_up, w_down):
    input_zero = start_latent.astype(jnp.bfloat16)
    pre_zero = block_sum(input_zero, w_up, True).astype(jnp.bfloat16)
    gelu_zero, slope_zero = gelu_parts(pre_zero.astype(jnp.float32))
    act_zero = gelu_zero.astype(jnp.bfloat16)
    latent_one = start_latent + jnp.dot(act_zero, w_down, preferred_element_type=jnp.float32)
    input_one = latent_one.astype(jnp.bfloat16)
    pre_one = block_sum(input_one, w_up, True).astype(jnp.bfloat16)
    gelu_one, slope_one = gelu_parts(pre_one.astype(jnp.float32))
    act_one = gelu_one.astype(jnp.bfloat16)
    error_two = target_two.astype(jnp.bfloat16)
    back_one = block_sum(error_two, w_down, False).astype(jnp.bfloat16)
    inner_one = (back_one.astype(jnp.float32) * slope_one).astype(jnp.bfloat16)
    grad_one = target_one + target_two + jnp.dot(inner_one, w_up.T, preferred_element_type=jnp.float32)
    error_one = grad_one.astype(jnp.bfloat16)
    back_zero = block_sum(error_one, w_down, False).astype(jnp.bfloat16)
    inner_zero = (back_zero.astype(jnp.float32) * slope_zero).astype(jnp.bfloat16)
    grad_start = grad_one + jnp.dot(inner_zero, w_up.T, preferred_element_type=jnp.float32)
    grad_up = jnp.dot(input_zero.T, inner_zero, preferred_element_type=jnp.float32) + jnp.dot(input_one.T, inner_one, preferred_element_type=jnp.float32)
    grad_down = jnp.dot(act_zero.T, error_one, preferred_element_type=jnp.float32) + jnp.dot(act_one.T, error_two, preferred_element_type=jnp.float32)
    return (grad_start, grad_up, grad_down)
```

```python
import math

import jax
import jax.numpy as jnp
from jax import lax
from jax.sharding import Mesh, PartitionSpec as P

gelu_scale = math.sqrt(2.0 / math.pi)
cubic_coef = 0.044715
f32 = jnp.float32
bf16 = jnp.bfloat16
SIZES = {"y": 4, "core": 2, "x": 4, "z": 8}
HIDDEN = ("x", "z")


def gelu_parts(preact):
    inner = gelu_scale * (preact + cubic_coef * preact * preact * preact)
    tangent = jnp.tanh(inner)
    value_out = 0.5 * preact * (1.0 + tangent)
    slope_out = 0.5 * (1.0 + tangent) + 0.5 * preact * (1.0 - tangent * tangent) * gelu_scale * (
        1.0 + 3.0 * cubic_coef * preact * preact
    )
    return (value_out, slope_out)


def swap(block):
    return lax.ppermute(block, "core", [(0, 1), (1, 0)])


def scatter_sum(parts, axes):
    landed = lax.all_to_all(parts, axes, 0, 0, tiled=True)
    return jnp.sum(landed.astype(f32), axis=0)


def spread(block, axes, count):
    copies = jnp.broadcast_to(block[None], (count,) + block.shape)
    return lax.all_to_all(copies, axes, 0, 0, tiled=True)


def dot(a, b):
    return jnp.dot(a, b, preferred_element_type=f32)


def dot_t(a, b):
    return lax.dot_general(a, b, (((1,), (1,)), ((), ())), preferred_element_type=f32)


def t_dot(a, b):
    return lax.dot_general(a, b, (((0,), (0,)), ((), ())), preferred_element_type=f32)


def shards(start_latent, target_one, target_two, w_up, w_down):
    n_y = SIZES["y"]
    n_h = SIZES["x"] * SIZES["z"]
    rows, wide = start_latent.shape
    deep = w_up.shape[1]
    eight = rows // (2 * n_h)
    half = rows // 2
    core = lax.axis_index("core")
    place = lax.axis_index("x") * SIZES["z"] + lax.axis_index("z")

    def halves(full):
        cut = full.reshape(n_h, 2, eight, wide)
        own = lax.dynamic_index_in_dim(cut, core, 1, keepdims=False)
        other = lax.dynamic_index_in_dim(cut, 1 - core, 1, keepdims=False)
        return own, other

    def own_rows(full):
        own, other = halves(full)
        mine = lax.dynamic_index_in_dim(own, place, 0, keepdims=False)
        theirs = lax.dynamic_index_in_dim(other, place, 0, keepdims=False)
        return jnp.concatenate([mine, swap(theirs)], axis=1)

    start_own, start_other = halves(start_latent)
    start_own = start_own.astype(bf16).reshape(half, wide)
    start_other = start_other.astype(bf16).reshape(half, wide)
    pre_other = dot(start_other, w_up).astype(bf16)
    pre_own = dot(start_own, w_up)
    pre_part = (pre_own + swap(pre_other).astype(f32)).astype(bf16)
    pre_zero = scatter_sum(pre_part.reshape(n_y, half // n_y, deep), "y").astype(bf16)
    gelu_zero, slope_zero = gelu_parts(pre_zero.astype(f32))
    act_zero = spread(gelu_zero.astype(bf16), "y", n_y).reshape(half, deep)

    up_wide = jnp.concatenate([w_up, swap(w_up)], axis=0)
    down_wide = jnp.concatenate([w_down, swap(w_down)], axis=1)

    down_part = dot(act_zero, down_wide).astype(bf16)
    latent_one = own_rows(start_latent) + scatter_sum(down_part.reshape(n_h, eight, 2 * wide), HIDDEN)
    input_one = spread(latent_one.astype(bf16), HIDDEN, n_h).reshape(half, 2 * wide)

    two_own, two_other = halves(target_two)
    two_own = two_own.astype(bf16).reshape(half, wide)
    two_other = two_other.astype(bf16).reshape(half, wide)
    back_other = dot_t(two_other, w_down).astype(bf16)
    back_own = dot_t(two_own, w_down)
    back_part = (back_own + swap(back_other).astype(f32)).astype(bf16)

    pre_part = dot(input_one, up_wide).astype(bf16)
    both = jnp.concatenate(
        [pre_part.reshape(n_y, half // n_y, deep), back_part.reshape(n_y, half // n_y, deep)], axis=2
    )
    both = scatter_sum(both, "y")
    pre_one = both[:, :deep].astype(bf16)
    back_one = both[:, deep:].astype(bf16)
    gelu_one, slope_one = gelu_parts(pre_one.astype(f32))
    act_one_part = gelu_one.astype(bf16)
    inner_one = (back_one.astype(f32) * slope_one).astype(bf16)
    inner_one = spread(inner_one, "y", n_y).reshape(half, deep)

    spread_part = dot_t(inner_one, up_wide).astype(bf16)
    targets = own_rows(target_one + target_two)
    grad_one = targets + scatter_sum(spread_part.reshape(n_h, eight, 2 * wide), HIDDEN)
    error_one = spread(grad_one.astype(bf16), HIDDEN, n_h).reshape(half, 2 * wide)
    grad_one_other = swap(grad_one[:, wide:])

    back_part = dot_t(error_one, down_wide).astype(bf16)
    back_zero = scatter_sum(back_part.reshape(n_y, half // n_y, deep), "y").astype(bf16)
    inner_zero = (back_zero.astype(f32) * slope_zero).astype(bf16)
    inner_zero = spread(inner_zero, "y", n_y).reshape(half, deep)
    inner_zero_other = swap(inner_zero)

    part_own = dot_t(inner_zero, w_up).astype(bf16).reshape(n_h, eight, wide)
    part_other = dot_t(inner_zero_other, w_up).astype(bf16).reshape(n_h, eight, wide)
    summed = scatter_sum(jnp.concatenate([part_own, part_other], axis=1), HIDDEN)
    grad_start = summed + jnp.concatenate([grad_one[:, :wide], grad_one_other], axis=0)
    grad_start = jnp.where(core == 0, grad_start, jnp.roll(grad_start, eight, axis=0))

    act_zero_other = swap(act_zero)
    act_one = lax.all_gather(act_one_part, "y", axis=0, tiled=True)
    act_one_other = swap(act_one)
    inner_one_other = swap(inner_one)
    input_one_other = swap(input_one[:, wide:])
    error_one_other = swap(error_one[:, wide:])

    grad_up = t_dot(
        jnp.concatenate([start_own, start_other, input_one[:, :wide], input_one_other], axis=0),
        jnp.concatenate([inner_zero, inner_zero_other, inner_one, inner_one_other], axis=0),
    )
    grad_down = t_dot(
        jnp.concatenate([act_zero, act_zero_other, act_one, act_one_other], axis=0),
        jnp.concatenate([error_one[:, :wide], error_one_other, two_own, two_other], axis=0),
    )
    return (grad_start, grad_up, grad_down)


def solution(mesh):
    fine = Mesh(
        mesh.devices.reshape(tuple(SIZES.values())), tuple(SIZES)
    )
    width, hidden = ("y", "core"), HIDDEN
    return jax.shard_map(
        shards,
        mesh=fine,
        in_specs=(
            P(None, width),
            P(None, width),
            P(None, width),
            P(width, hidden),
            P(hidden, width),
        ),
        out_specs=(P(hidden, width), P(width, hidden), P(hidden, width)),
        check_vma=False,
    )
```

```python
import functools
import math

import jax
import jax.numpy as jnp
from jax import lax
from jax.experimental import pallas as pl
from jax.experimental.pallas import tpu as pltpu
from jax.sharding import Mesh, PartitionSpec as P

gelu_scale = math.sqrt(2.0 / math.pi)
cubic_coef = 0.044715
f32 = jnp.float32
bf16 = jnp.bfloat16
SIZES = {"y": 4, "core": 2, "x": 4, "z": 8}
HIDDEN = ("x", "z")
STRIP = 64


def gelu_parts(preact):
    inner = gelu_scale * (preact + cubic_coef * preact * preact * preact)
    tangent = jnp.tanh(inner)
    value_out = 0.5 * preact * (1.0 + tangent)
    slope_out = 0.5 * (1.0 + tangent) + 0.5 * preact * (1.0 - tangent * tangent) * gelu_scale * (
        1.0 + 3.0 * cubic_coef * preact * preact
    )
    return (value_out, slope_out)


def dot(a, b):
    return jnp.dot(a, b, preferred_element_type=f32)


def dot_t(a, b):
    return lax.dot_general(a, b, (((1,), (1,)), ((), ())), preferred_element_type=f32)


def t_dot(a, b):
    return lax.dot_general(a, b, (((0,), (0,)), ((), ())), preferred_element_type=f32)


def call(body, outs, *operands, flops=0):
    size = sum(math.prod(o.shape) * o.dtype.itemsize for o in operands)
    size += sum(math.prod(s) * jnp.dtype(t).itemsize for s, t in outs)
    got = pl.pallas_call(
        body,
        out_shape=[jax.ShapeDtypeStruct(s, t) for s, t in outs],
        in_specs=[pl.BlockSpec(memory_space=pltpu.VMEM)] * len(operands),
        out_specs=[pl.BlockSpec(memory_space=pltpu.VMEM)] * len(outs),
        cost_estimate=pl.CostEstimate(flops=flops, bytes_accessed=size, transcendentals=0),
        compiler_params=pltpu.CompilerParams(vmem_limit_bytes=24 * 2**20),
    )(*operands)
    return got[0] if len(outs) == 1 else got


def widen(product, rows_deep, own_block, other_block):
    rows, wide = rows_deep.shape[0], rows_deep.shape[1]

    def body(x_ref, a_ref, b_ref, o_ref):
        o_ref[:, :wide] = product(x_ref[...], a_ref[...]).astype(bf16)
        o_ref[:, wide:] = product(x_ref[...], b_ref[...]).astype(bf16)

    return call(
        body, [((rows, 2 * wide), bf16)], rows_deep, own_block, other_block, flops=4 * rows * wide * wide
    )


def narrow(product, rows_wide, own_block, other_block):
    rows, wide = rows_wide.shape[0], rows_wide.shape[1] // 2

    def body(x_ref, a_ref, b_ref, o_ref):
        total = product(x_ref[:, :wide], a_ref[...]) + product(x_ref[:, wide:], b_ref[...])
        o_ref[...] = total.astype(bf16)

    return call(
        body, [((rows, wide), bf16)], rows_wide, own_block, other_block, flops=4 * rows * wide * wide
    )


def add_up(ref, columns):
    total = ref[0, :, columns].astype(f32)
    for k in range(1, ref.shape[0]):
        total = total + ref[k, :, columns].astype(f32)
    return total


def strips(width, step):
    return [slice(first, first + step) for first in range(0, width, step)]


def sum_and_copy(landed, added):
    count, eight, wide = landed.shape

    def body(l_ref, a_ref, s_ref, c_ref):
        for cols in strips(wide, 256):
            total = a_ref[:, cols] + add_up(l_ref, cols)
            s_ref[:, cols] = total
            rounded = total.astype(bf16)
            for k in range(count):
                c_ref[k, :, cols] = rounded

    return call(body, [((eight, wide), f32), ((count, eight, wide), bf16)], landed, added)


def sum_last(landed, added):
    count, eight, wide = landed.shape
    half = wide // 2

    def body(l_ref, a_ref, m_ref, t_ref):
        for cols in strips(half, 256):
            m_ref[:, cols] = a_ref[:, cols] + add_up(l_ref, cols)
            far = slice(cols.start + half, cols.stop + half)
            t_ref[:, cols] = a_ref[:, far] + add_up(l_ref, far)

    return call(body, [((eight, half), f32)] * 2, landed, added)


def activate(landed):
    count, rows, deep = landed.shape

    def body(l_ref, p_ref, c_ref):
        for cols in strips(deep, 128):
            pre = add_up(l_ref, cols).astype(bf16)
            p_ref[:, cols] = pre
            value = gelu_parts(pre.astype(f32))[0].astype(bf16)
            for k in range(count):
                c_ref[k, :, cols] = value

    return call(body, [((rows, deep), bf16), ((count, rows, deep), bf16)], landed)


def activate_and_back(landed):
    count, rows, deep = landed.shape[0], landed.shape[1], landed.shape[2] // 2

    def body(l_ref, v_ref, c_ref):
        for cols in strips(deep, 128):
            pre = add_up(l_ref, cols).astype(bf16)
            value, slope = gelu_parts(pre.astype(f32))
            v_ref[:, cols] = value.astype(bf16)
            back = add_up(l_ref, slice(cols.start + deep, cols.stop + deep)).astype(bf16)
            inner = (back.astype(f32) * slope).astype(bf16)
            for k in range(count):
                c_ref[k, :, cols] = inner

    return call(body, [((rows, deep), bf16), ((count, rows, deep), bf16)], landed)


def back_through(landed, pre):
    count, rows, deep = landed.shape

    def body(l_ref, p_ref, c_ref):
        for cols in strips(deep, 128):
            slope = gelu_parts(p_ref[:, cols].astype(f32))[1]
            back = add_up(l_ref, cols).astype(bf16)
            inner = (back.astype(f32) * slope).astype(bf16)
            for k in range(count):
                c_ref[k, :, cols] = inner

    return call(body, [((count, rows, deep), bf16)], landed, pre)


def swap(block):
    return lax.ppermute(block, "core", [(0, 1), (1, 0)])


def exchange(parts, axes):
    return lax.all_to_all(parts, axes, 0, 0, tiled=True)


def shards(start_latent, target_one, target_two, w_up, w_down):
    n_y = SIZES["y"]
    n_h = SIZES["x"] * SIZES["z"]
    rows, wide = start_latent.shape
    deep = w_up.shape[1]
    eight = rows // (2 * n_h)
    half = rows // 2
    quarter = half // n_y
    core = lax.axis_index("core")
    place = lax.axis_index("x") * SIZES["z"] + lax.axis_index("z")

    def halves(full):
        cut = full.reshape(n_h, 2, eight, wide)
        own = lax.dynamic_index_in_dim(cut, core, 1, keepdims=False)
        other = lax.dynamic_index_in_dim(cut, 1 - core, 1, keepdims=False)
        return own, other

    def own_rows(full):
        own, other = halves(full)
        mine = lax.dynamic_index_in_dim(own, place, 0, keepdims=False)
        theirs = lax.dynamic_index_in_dim(other, place, 0, keepdims=False)
        return jnp.concatenate([mine, swap(theirs)], axis=1)

    def rounded_halves(full):
        own, other = halves(full)
        return own.astype(bf16).reshape(half, wide), other.astype(bf16).reshape(half, wide)

    def both_cores(own, other_part):
        return (own + swap(other_part.astype(bf16)).astype(f32)).astype(bf16)

    up_other = swap(w_up)
    down_other = swap(w_down)

    start_own, start_other = rounded_halves(start_latent)
    pre_part = both_cores(dot(start_own, w_up), dot(start_other, w_up))
    pre_zero, act_zero = activate(exchange(pre_part.reshape(n_y, quarter, deep), "y"))
    act_zero = exchange(act_zero, "y").reshape(half, deep)

    part = widen(dot, act_zero, w_down, down_other)
    latent_one, input_one = sum_and_copy(
        exchange(part.reshape(n_h, eight, 2 * wide), HIDDEN), own_rows(start_latent)
    )
    input_one = exchange(input_one, HIDDEN).reshape(half, 2 * wide)

    two_own, two_other = rounded_halves(target_two)
    back_part = both_cores(dot_t(two_own, w_down), dot_t(two_other, w_down))

    pre_part = narrow(dot, input_one, w_up, up_other)
    both = jnp.concatenate([pre_part.reshape(n_y, quarter, deep), back_part.reshape(n_y, quarter, deep)], axis=2)
    act_one, inner_one = activate_and_back(exchange(both, "y"))
    inner_one = exchange(inner_one, "y").reshape(half, deep)

    part = widen(dot_t, inner_one, w_up, up_other)
    grad_one, error_one = sum_and_copy(
        exchange(part.reshape(n_h, eight, 2 * wide), HIDDEN), own_rows(target_one + target_two)
    )
    error_one = exchange(error_one, HIDDEN).reshape(half, 2 * wide)

    back_part = narrow(dot_t, error_one, w_down, down_other)
    inner_zero = back_through(exchange(back_part.reshape(n_y, quarter, deep), "y"), pre_zero)
    inner_zero = exchange(inner_zero, "y").reshape(half, deep)

    part = widen(dot_t, inner_zero, w_up, up_other)
    landed = exchange(part.reshape(n_h, eight, 2 * wide), HIDDEN)

    act_one = lax.all_gather(act_one, "y", axis=0, tiled=True)
    grad_down = t_dot(
        jnp.concatenate([act_zero, swap(act_zero), act_one, swap(act_one)], axis=0),
        jnp.concatenate([error_one[:, :wide], swap(error_one[:, wide:]), two_own, two_other], axis=0),
    )
    grad_up = t_dot(
        jnp.concatenate([start_own, start_other, input_one[:, :wide], swap(input_one[:, wide:])], axis=0),
        jnp.concatenate([inner_zero, swap(inner_zero), inner_one, swap(inner_one)], axis=0),
    )
    landed, grad_up, grad_down = lax.optimization_barrier((landed, grad_up, grad_down))

    mine, theirs = sum_last(landed, grad_one)
    theirs = swap(theirs)
    grad_start = jnp.where(
        core == 0, jnp.concatenate([mine, theirs], axis=0), jnp.concatenate([theirs, mine], axis=0)
    )
    return (grad_start, grad_up, grad_down)


def solution(mesh):
    fine = Mesh(mesh.devices.reshape(tuple(SIZES.values())), tuple(SIZES))
    width, hidden = ("y", "core"), HIDDEN
    return jax.shard_map(
        shards,
        mesh=fine,
        in_specs=(
            P(None, width),
            P(None, width),
            P(None, width),
            P(width, hidden),
            P(hidden, width),
        ),
        out_specs=(P(hidden, width), P(width, hidden), P(hidden, width)),
        check_vma=False,
    )
```

```python
import functools
import math

import jax
import jax.numpy as jnp
from jax import lax
from jax.experimental import pallas as pl
from jax.experimental.pallas import tpu as pltpu
from jax.sharding import Mesh, PartitionSpec as P

gelu_scale = math.sqrt(2.0 / math.pi)
cubic_coef = 0.044715
f32 = jnp.float32
bf16 = jnp.bfloat16
SIZES = {"y": 4, "core": 2, "x": 4, "z": 8}
HIDDEN = ("x", "z")
STRIP = 64


def gelu_parts(preact):
    inner = gelu_scale * (preact + cubic_coef * preact * preact * preact)
    tangent = jnp.tanh(inner)
    value_out = 0.5 * preact * (1.0 + tangent)
    slope_out = 0.5 * (1.0 + tangent) + 0.5 * preact * (1.0 - tangent * tangent) * gelu_scale * (
        1.0 + 3.0 * cubic_coef * preact * preact
    )
    return (value_out, slope_out)


def dot(a, b):
    return jnp.dot(a, b, preferred_element_type=f32)


def dot_t(a, b):
    return lax.dot_general(a, b, (((1,), (1,)), ((), ())), preferred_element_type=f32)


def t_dot(a, b):
    return lax.dot_general(a, b, (((0,), (0,)), ((), ())), preferred_element_type=f32)


def call(body, outs, *operands, flops=0):
    size = sum(math.prod(o.shape) * o.dtype.itemsize for o in operands)
    size += sum(math.prod(s) * jnp.dtype(t).itemsize for s, t in outs)
    got = pl.pallas_call(
        body,
        out_shape=[jax.ShapeDtypeStruct(s, t) for s, t in outs],
        in_specs=[pl.BlockSpec(memory_space=pltpu.VMEM)] * len(operands),
        out_specs=[pl.BlockSpec(memory_space=pltpu.VMEM)] * len(outs),
        cost_estimate=pl.CostEstimate(flops=flops, bytes_accessed=size, transcendentals=0),
        compiler_params=pltpu.CompilerParams(vmem_limit_bytes=24 * 2**20),
    )(*operands)
    return got[0] if len(outs) == 1 else got


def widen(product, rows_deep, own_block, other_block):
    rows, wide = rows_deep.shape[0], rows_deep.shape[1]

    def body(x_ref, a_ref, b_ref, o_ref):
        o_ref[:, :wide] = product(x_ref[...], a_ref[...]).astype(bf16)
        o_ref[:, wide:] = product(x_ref[...], b_ref[...]).astype(bf16)

    return call(
        body, [((rows, 2 * wide), bf16)], rows_deep, own_block, other_block, flops=4 * rows * wide * wide
    )


def narrow(product, rows_wide, own_block, other_block):
    rows, wide = rows_wide.shape[0], rows_wide.shape[1] // 2

    def body(x_ref, a_ref, b_ref, o_ref):
        total = product(x_ref[:, :wide], a_ref[...]) + product(x_ref[:, wide:], b_ref[...])
        o_ref[...] = total.astype(bf16)

    return call(
        body, [((rows, wide), bf16)], rows_wide, own_block, other_block, flops=4 * rows * wide * wide
    )


def add_up(ref, columns):
    total = ref[0, :, columns].astype(f32)
    for k in range(1, ref.shape[0]):
        total = total + ref[k, :, columns].astype(f32)
    return total


def strips(width, step):
    return [slice(first, first + step) for first in range(0, width, step)]


def sum_and_copy(landed, added):
    count, eight, wide = landed.shape

    def body(l_ref, a_ref, s_ref, c_ref):
        for cols in strips(wide, 256):
            total = a_ref[:, cols] + add_up(l_ref, cols)
            s_ref[:, cols] = total
            rounded = total.astype(bf16)
            for k in range(count):
                c_ref[k, :, cols] = rounded

    return call(body, [((eight, wide), f32), ((count, eight, wide), bf16)], landed, added)


def sum_last(landed, added):
    count, eight, wide = landed.shape
    half = wide // 2

    def body(l_ref, a_ref, m_ref, t_ref):
        for cols in strips(half, 256):
            m_ref[:, cols] = a_ref[:, cols] + add_up(l_ref, cols)
            far = slice(cols.start + half, cols.stop + half)
            t_ref[:, cols] = a_ref[:, far] + add_up(l_ref, far)

    return call(body, [((eight, half), f32)] * 2, landed, added)


def activate(landed):
    count, rows, deep = landed.shape

    def body(l_ref, p_ref, c_ref):
        for cols in strips(deep, 128):
            pre = add_up(l_ref, cols).astype(bf16)
            p_ref[:, cols] = pre
            value = gelu_parts(pre.astype(f32))[0].astype(bf16)
            for k in range(count):
                c_ref[k, :, cols] = value

    return call(body, [((rows, deep), bf16), ((count, rows, deep), bf16)], landed)


def activate_and_back(landed):
    count, rows, deep = landed.shape[0], landed.shape[1], landed.shape[2] // 2

    def body(l_ref, v_ref, c_ref):
        for cols in strips(deep, 128):
            pre = add_up(l_ref, cols).astype(bf16)
            value, slope = gelu_parts(pre.astype(f32))
            v_ref[:, cols] = value.astype(bf16)
            back = add_up(l_ref, slice(cols.start + deep, cols.stop + deep)).astype(bf16)
            inner = (back.astype(f32) * slope).astype(bf16)
            for k in range(count):
                c_ref[k, :, cols] = inner

    return call(body, [((rows, deep), bf16), ((count, rows, deep), bf16)], landed)


def back_through(landed, pre):
    count, rows, deep = landed.shape

    def body(l_ref, p_ref, c_ref):
        for cols in strips(deep, 128):
            slope = gelu_parts(p_ref[:, cols].astype(f32))[1]
            back = add_up(l_ref, cols).astype(bf16)
            inner = (back.astype(f32) * slope).astype(bf16)
            for k in range(count):
                c_ref[k, :, cols] = inner

    return call(body, [((count, rows, deep), bf16)], landed, pre)


def swap(block):
    return lax.ppermute(block, "core", [(0, 1), (1, 0)])


def exchange(parts, axes):
    return lax.all_to_all(parts, axes, 0, 0, tiled=True)


def shards(start_latent, target_one, target_two, w_up, w_down):
    n_y = SIZES["y"]
    n_h = SIZES["x"] * SIZES["z"]
    rows, wide = start_latent.shape
    deep = w_up.shape[1]
    eight = rows // (2 * n_h)
    half = rows // 2
    quarter = half // n_y
    core = lax.axis_index("core")
    place = lax.axis_index("x") * SIZES["z"] + lax.axis_index("z")

    def halves(full):
        cut = full.reshape(n_h, 2, eight, wide)
        own = lax.dynamic_index_in_dim(cut, core, 1, keepdims=False)
        other = lax.dynamic_index_in_dim(cut, 1 - core, 1, keepdims=False)
        return own, other

    def own_rows(*terms):
        first = 2 * eight * place
        pair = sum(lax.dynamic_slice_in_dim(full, first, 2 * eight, 0) for full in terms)
        mine = lax.dynamic_slice_in_dim(pair, eight * core, eight, 0)
        theirs = lax.dynamic_slice_in_dim(pair, eight * (1 - core), eight, 0)
        return jnp.concatenate([mine, swap(theirs)], axis=1)

    def rounded_halves(full):
        own, other = halves(full)
        return own.astype(bf16).reshape(half, wide), other.astype(bf16).reshape(half, wide)

    def both_cores(own, other_part):
        return (own + swap(other_part.astype(bf16)).astype(f32)).astype(bf16)

    up_other = swap(w_up)
    down_other = swap(w_down)

    start_own, start_other = rounded_halves(start_latent)
    pre_part = both_cores(dot(start_own, w_up), dot(start_other, w_up))
    pre_zero, act_zero = activate(exchange(pre_part.reshape(n_y, quarter, deep), "y"))
    act_zero = exchange(act_zero, "y").reshape(half, deep)

    part = widen(dot, act_zero, w_down, down_other)
    latent_one, input_one = sum_and_copy(
        exchange(part.reshape(n_h, eight, 2 * wide), HIDDEN), own_rows(start_latent)
    )
    input_one = exchange(input_one, HIDDEN).reshape(half, 2 * wide)

    two_own, two_other = rounded_halves(target_two)
    back_part = both_cores(dot_t(two_own, w_down), dot_t(two_other, w_down))

    pre_part = narrow(dot, input_one, w_up, up_other)
    both = jnp.concatenate([pre_part.reshape(n_y, quarter, deep), back_part.reshape(n_y, quarter, deep)], axis=2)
    act_one, inner_one = activate_and_back(exchange(both, "y"))
    inner_one = exchange(inner_one, "y").reshape(half, deep)

    part = widen(dot_t, inner_one, w_up, up_other)
    landed = exchange(part.reshape(n_h, eight, 2 * wide), HIDDEN)
    act_one = lax.all_gather(act_one, "y", axis=0, tiled=True)
    landed, act_one = lax.optimization_barrier((landed, act_one))
    grad_one, error_one = sum_and_copy(landed, own_rows(target_one, target_two))
    error_one = exchange(error_one, HIDDEN).reshape(half, 2 * wide)
    grad_up = t_dot(
        jnp.concatenate([input_one[:, :wide], swap(input_one[:, wide:])], axis=0),
        jnp.concatenate([inner_one, swap(inner_one)], axis=0),
    )
    grad_down = t_dot(
        jnp.concatenate([act_one, swap(act_one)], axis=0), jnp.concatenate([two_own, two_other], axis=0)
    )
    act_zero_other = swap(act_zero)
    error_one, grad_up, grad_down, act_zero_other = lax.optimization_barrier(
        (error_one, grad_up, grad_down, act_zero_other)
    )

    back_part = narrow(dot_t, error_one, w_down, down_other)
    inner_zero = back_through(exchange(back_part.reshape(n_y, quarter, deep), "y"), pre_zero)
    inner_zero = exchange(inner_zero, "y").reshape(half, deep)

    part = widen(dot_t, inner_zero, w_up, up_other)
    landed = exchange(part.reshape(n_h, eight, 2 * wide), HIDDEN)

    grad_down = grad_down + t_dot(
        jnp.concatenate([act_zero, act_zero_other], axis=0),
        jnp.concatenate([error_one[:, :wide], swap(error_one[:, wide:])], axis=0),
    )
    grad_up = grad_up + t_dot(
        jnp.concatenate([start_own, start_other], axis=0),
        jnp.concatenate([inner_zero, swap(inner_zero)], axis=0),
    )
    landed, grad_up, grad_down = lax.optimization_barrier((landed, grad_up, grad_down))

    mine, theirs = sum_last(landed, grad_one)
    theirs = swap(theirs)
    grad_start = jnp.where(
        core == 0, jnp.concatenate([mine, theirs], axis=0), jnp.concatenate([theirs, mine], axis=0)
    )
    return (grad_start, grad_up, grad_down)


def solution(mesh):
    fine = Mesh(mesh.devices.reshape(tuple(SIZES.values())), tuple(SIZES))
    width, hidden = ("y", "core"), HIDDEN
    return jax.shard_map(
        shards,
        mesh=fine,
        in_specs=(
            P(None, width),
            P(None, width),
            P(None, width),
            P(width, hidden),
            P(hidden, width),
        ),
        out_specs=(P(hidden, width), P(width, hidden), P(hidden, width)),
        check_vma=False,
    )
```

```python
import functools
import math

import jax
import jax.numpy as jnp
from jax import lax
from jax.experimental import pallas as pl
from jax.experimental.pallas import tpu as pltpu
from jax.sharding import Mesh, PartitionSpec as P

gelu_scale = math.sqrt(2.0 / math.pi)
cubic_coef = 0.044715
f32 = jnp.float32
bf16 = jnp.bfloat16
SIZES = {"y": 4, "core": 2, "x": 4, "z": 8}
HIDDEN = ("x", "z")
STRIP = 64


def gelu_parts(preact):
    inner = gelu_scale * (preact + cubic_coef * preact * preact * preact)
    tangent = jnp.tanh(inner)
    value_out = 0.5 * preact * (1.0 + tangent)
    slope_out = 0.5 * (1.0 + tangent) + 0.5 * preact * (1.0 - tangent * tangent) * gelu_scale * (
        1.0 + 3.0 * cubic_coef * preact * preact
    )
    return (value_out, slope_out)


def dot(a, b):
    return jnp.dot(a, b, preferred_element_type=f32)


def dot_t(a, b):
    return lax.dot_general(a, b, (((1,), (1,)), ((), ())), preferred_element_type=f32)


def t_dot(a, b):
    return lax.dot_general(a, b, (((0,), (0,)), ((), ())), preferred_element_type=f32)


def call(body, outs, *operands, flops=0):
    size = sum(math.prod(o.shape) * o.dtype.itemsize for o in operands)
    size += sum(math.prod(s) * jnp.dtype(t).itemsize for s, t in outs)
    got = pl.pallas_call(
        body,
        out_shape=[jax.ShapeDtypeStruct(s, t) for s, t in outs],
        in_specs=[pl.BlockSpec(memory_space=pltpu.VMEM)] * len(operands),
        out_specs=[pl.BlockSpec(memory_space=pltpu.VMEM)] * len(outs),
        cost_estimate=pl.CostEstimate(flops=flops, bytes_accessed=size, transcendentals=0),
        compiler_params=pltpu.CompilerParams(vmem_limit_bytes=24 * 2**20),
    )(*operands)
    return got[0] if len(outs) == 1 else got


def widen(product, rows_deep, own_block, other_block):
    rows, wide = rows_deep.shape[0], own_block.shape[0]

    def body(x_ref, a_ref, b_ref, o_ref):
        o_ref[:, :wide] = product(x_ref[:, :wide], a_ref[...]).astype(bf16)
        o_ref[:, wide:] = product(x_ref[:, :wide], b_ref[...]).astype(bf16)

    return call(
        body, [((rows, 2 * wide), bf16)], rows_deep, own_block, other_block, flops=4 * rows * wide * wide
    )


def narrow(product, rows_wide, own_block, other_block):
    rows, wide = rows_wide.shape[0], rows_wide.shape[1] // 2

    def body(x_ref, a_ref, b_ref, o_ref):
        total = product(x_ref[:, :wide], a_ref[...]) + product(x_ref[:, wide:], b_ref[...])
        o_ref[...] = total.astype(bf16)

    return call(
        body, [((rows, wide), bf16)], rows_wide, own_block, other_block, flops=4 * rows * wide * wide
    )


def add_up(ref, columns):
    total = ref[0, :, columns].astype(f32)
    for k in range(1, ref.shape[0]):
        total = total + ref[k, :, columns].astype(f32)
    return total


def strips(width, step):
    return [slice(first, first + step) for first in range(0, width, step)]


def sum_and_copy(landed, added):
    count, eight, wide = landed.shape

    def body(l_ref, a_ref, s_ref, c_ref):
        for cols in strips(wide, 256):
            total = a_ref[:, cols] + add_up(l_ref, cols)
            s_ref[:, cols] = total
            rounded = total.astype(bf16)
            for k in range(count):
                c_ref[k, :, cols] = rounded

    return call(body, [((eight, wide), f32), ((count, eight, wide), bf16)], landed, added)


def sum_last(landed, added):
    count, eight, wide = landed.shape
    half = wide // 2

    def body(l_ref, a_ref, m_ref, t_ref):
        for cols in strips(half, 256):
            m_ref[:, cols] = a_ref[:, cols] + add_up(l_ref, cols)
            far = slice(cols.start + half, cols.stop + half)
            t_ref[:, cols] = a_ref[:, far] + add_up(l_ref, far)

    return call(body, [((eight, half), f32)] * 2, landed, added)


def activate(landed):
    count, rows, deep = landed.shape

    def body(l_ref, p_ref, c_ref):
        for cols in strips(deep, 128):
            pre = add_up(l_ref, cols).astype(bf16)
            p_ref[:, cols] = pre
            value = gelu_parts(pre.astype(f32))[0].astype(bf16)
            for k in range(count):
                c_ref[k, :, cols] = value

    return call(body, [((rows, deep), bf16), ((count, rows, deep), bf16)], landed)


def activate_and_back(landed):
    count, rows, deep = landed.shape[0], landed.shape[1], landed.shape[2] // 2

    def body(l_ref, c_ref):
        for cols in strips(deep, 128):
            far = slice(cols.start + deep, cols.stop + deep)
            pre = add_up(l_ref, cols).astype(bf16)
            value, slope = gelu_parts(pre.astype(f32))
            value = value.astype(bf16)
            back = add_up(l_ref, far).astype(bf16)
            inner = (back.astype(f32) * slope).astype(bf16)
            for k in range(count):
                c_ref[k, :, cols] = inner
                c_ref[k, :, far] = value

    return call(body, [(landed.shape, bf16)], landed)


def back_through(landed, pre):
    count, rows, deep = landed.shape

    def body(l_ref, p_ref, c_ref):
        for cols in strips(deep, 128):
            slope = gelu_parts(p_ref[:, cols].astype(f32))[1]
            back = add_up(l_ref, cols).astype(bf16)
            inner = (back.astype(f32) * slope).astype(bf16)
            for k in range(count):
                c_ref[k, :, cols] = inner

    return call(body, [((count, rows, deep), bf16)], landed, pre)


def swap(block):
    return lax.ppermute(block, "core", [(0, 1), (1, 0)])


def exchange(parts, axes):
    return lax.all_to_all(parts, axes, 0, 0, tiled=True)


def shards(start_latent, target_one, target_two, w_up, w_down):
    n_y = SIZES["y"]
    n_h = SIZES["x"] * SIZES["z"]
    rows, wide = start_latent.shape
    deep = w_up.shape[1]
    eight = rows // (2 * n_h)
    half = rows // 2
    quarter = half // n_y
    core = lax.axis_index("core")
    place = lax.axis_index("x") * SIZES["z"] + lax.axis_index("z")

    def halves(full):
        cut = full.reshape(n_h, 2, eight, wide)
        own = lax.dynamic_index_in_dim(cut, core, 1, keepdims=False)
        other = lax.dynamic_index_in_dim(cut, 1 - core, 1, keepdims=False)
        return own, other

    def own_rows(*terms):
        first = 2 * eight * place
        pair = sum(lax.dynamic_slice_in_dim(full, first, 2 * eight, 0) for full in terms)
        mine = lax.dynamic_slice_in_dim(pair, eight * core, eight, 0)
        theirs = lax.dynamic_slice_in_dim(pair, eight * (1 - core), eight, 0)
        return jnp.concatenate([mine, swap(theirs)], axis=1)

    def rounded_halves(full):
        own, other = halves(full)
        return own.astype(bf16).reshape(half, wide), other.astype(bf16).reshape(half, wide)

    def both_cores(own, other_part):
        return (own + swap(other_part.astype(bf16)).astype(f32)).astype(bf16)

    down_other = swap(w_down)

    start_own, start_other = rounded_halves(start_latent)
    pre_part = both_cores(dot(start_own, w_up), dot(start_other, w_up))
    pre_zero, act_zero = activate(exchange(pre_part.reshape(n_y, quarter, deep), "y"))
    act_zero = exchange(act_zero, "y").reshape(half, deep)

    part = widen(dot, act_zero, w_down, down_other)
    landed = exchange(part.reshape(n_h, eight, 2 * wide), HIDDEN)
    up_other = swap(w_up)
    two_own, two_other = rounded_halves(target_two)
    back_part = both_cores(dot_t(two_own, w_down), dot_t(two_other, w_down))
    start_rows = own_rows(start_latent)
    target_rows = own_rows(target_one, target_two)
    landed, up_other, back_part, start_rows, target_rows = lax.optimization_barrier(
        (landed, up_other, back_part, start_rows, target_rows)
    )
    latent_one, input_one = sum_and_copy(landed, start_rows)
    input_one = exchange(input_one, HIDDEN).reshape(half, 2 * wide)

    pre_part = narrow(dot, input_one, w_up, up_other)
    both = jnp.concatenate([pre_part.reshape(n_y, quarter, deep), back_part.reshape(n_y, quarter, deep)], axis=2)
    one = activate_and_back(exchange(both, "y"))
    one = exchange(one, "y").reshape(half, 2 * deep)

    part = widen(dot_t, one, w_up, up_other)
    landed = exchange(part.reshape(n_h, eight, 2 * wide), HIDDEN)
    one_other = swap(one)
    input_far = swap(input_one[:, wide:])
    act_zero_other = swap(act_zero)
    grad_up = t_dot(
        jnp.concatenate([input_one[:, :wide], input_far], axis=0),
        jnp.concatenate([one[:, :deep], one_other[:, :deep]], axis=0),
    )
    grad_down = t_dot(
        jnp.concatenate([one[:, deep:], one_other[:, deep:]], axis=0),
        jnp.concatenate([two_own, two_other], axis=0),
    )
    landed, grad_up, grad_down, act_zero_other = lax.optimization_barrier(
        (landed, grad_up, grad_down, act_zero_other)
    )
    grad_one, error_one = sum_and_copy(landed, target_rows)
    error_one = exchange(error_one, HIDDEN).reshape(half, 2 * wide)

    back_part = narrow(dot_t, error_one, w_down, down_other)
    inner_zero = back_through(exchange(back_part.reshape(n_y, quarter, deep), "y"), pre_zero)
    inner_zero = exchange(inner_zero, "y").reshape(half, deep)

    part = widen(dot_t, inner_zero, w_up, up_other)
    landed = exchange(part.reshape(n_h, eight, 2 * wide), HIDDEN)

    grad_down = grad_down + t_dot(
        jnp.concatenate([act_zero, act_zero_other], axis=0),
        jnp.concatenate([error_one[:, :wide], swap(error_one[:, wide:])], axis=0),
    )
    grad_up = grad_up + t_dot(
        jnp.concatenate([start_own, start_other], axis=0),
        jnp.concatenate([inner_zero, swap(inner_zero)], axis=0),
    )
    landed, grad_up, grad_down = lax.optimization_barrier((landed, grad_up, grad_down))

    mine, theirs = sum_last(landed, grad_one)
    theirs = swap(theirs)
    grad_start = jnp.where(
        core == 0, jnp.concatenate([mine, theirs], axis=0), jnp.concatenate([theirs, mine], axis=0)
    )
    return (grad_start, grad_up, grad_down)


def solution(mesh):
    fine = Mesh(mesh.devices.reshape(tuple(SIZES.values())), tuple(SIZES))
    width, hidden = ("y", "core"), HIDDEN
    return jax.shard_map(
        shards,
        mesh=fine,
        in_specs=(
            P(None, width),
            P(None, width),
            P(None, width),
            P(width, hidden),
            P(hidden, width),
        ),
        out_specs=(P(hidden, width), P(width, hidden), P(hidden, width)),
        check_vma=False,
    )
```

```python
import functools
import math

import jax
import jax.numpy as jnp
from jax import lax
from jax.experimental import pallas as pl
from jax.experimental.pallas import tpu as pltpu
from jax.sharding import Mesh, PartitionSpec as P

gelu_scale = math.sqrt(2.0 / math.pi)
cubic_coef = 0.044715
f32 = jnp.float32
bf16 = jnp.bfloat16
SIZES = {"y": 4, "core": 2, "x": 4, "z": 8}
HIDDEN = ("x", "z")
STRIP = 64


def gelu_parts(preact):
    inner = gelu_scale * (preact + cubic_coef * preact * preact * preact)
    tangent = jnp.tanh(inner)
    value_out = 0.5 * preact * (1.0 + tangent)
    slope_out = 0.5 * (1.0 + tangent) + 0.5 * preact * (1.0 - tangent * tangent) * gelu_scale * (
        1.0 + 3.0 * cubic_coef * preact * preact
    )
    return (value_out, slope_out)


def dot(a, b):
    return jnp.dot(a, b, preferred_element_type=f32)


def dot_t(a, b):
    return lax.dot_general(a, b, (((1,), (1,)), ((), ())), preferred_element_type=f32)


def t_dot(a, b):
    return lax.dot_general(a, b, (((0,), (0,)), ((), ())), preferred_element_type=f32)


def call(body, outs, *operands, flops=0):
    size = sum(math.prod(o.shape) * o.dtype.itemsize for o in operands)
    size += sum(math.prod(s) * jnp.dtype(t).itemsize for s, t in outs)
    got = pl.pallas_call(
        body,
        out_shape=[jax.ShapeDtypeStruct(s, t) for s, t in outs],
        in_specs=[pl.BlockSpec(memory_space=pltpu.VMEM)] * len(operands),
        out_specs=[pl.BlockSpec(memory_space=pltpu.VMEM)] * len(outs),
        cost_estimate=pl.CostEstimate(flops=flops, bytes_accessed=size, transcendentals=0),
        compiler_params=pltpu.CompilerParams(vmem_limit_bytes=24 * 2**20),
    )(*operands)
    return got[0] if len(outs) == 1 else got


def widen(product, rows_deep, own_block, other_block):
    rows, wide = rows_deep.shape[0], own_block.shape[0]

    def body(x_ref, a_ref, b_ref, o_ref):
        o_ref[:, :wide] = product(x_ref[:, :wide], a_ref[...]).astype(bf16)
        o_ref[:, wide:] = product(x_ref[:, :wide], b_ref[...]).astype(bf16)

    return call(
        body, [((rows, 2 * wide), bf16)], rows_deep, own_block, other_block, flops=4 * rows * wide * wide
    )


def narrow(product, rows_wide, own_block, other_block):
    rows, wide = rows_wide.shape[0], rows_wide.shape[1] // 2

    def body(x_ref, a_ref, b_ref, o_ref):
        total = product(x_ref[:, :wide], a_ref[...]) + product(x_ref[:, wide:], b_ref[...])
        o_ref[...] = total.astype(bf16)

    return call(
        body, [((rows, wide), bf16)], rows_wide, own_block, other_block, flops=4 * rows * wide * wide
    )


def add_up(ref, columns):
    total = ref[0, :, columns].astype(f32)
    for k in range(1, ref.shape[0]):
        total = total + ref[k, :, columns].astype(f32)
    return total


def strips(width, step):
    return [slice(first, first + step) for first in range(0, width, step)]


def sum_and_copy(landed, added):
    count, eight, wide = landed.shape

    def body(l_ref, a_ref, s_ref, c_ref):
        for cols in strips(wide, 256):
            total = a_ref[:, cols] + add_up(l_ref, cols)
            s_ref[:, cols] = total
            rounded = total.astype(bf16)
            for k in range(count):
                c_ref[k, :, cols] = rounded

    return call(body, [((eight, wide), f32), ((count, eight, wide), bf16)], landed, added)


def sum_last(landed, added):
    count, eight, wide = landed.shape
    half = wide // 2

    def body(l_ref, a_ref, m_ref, t_ref):
        for cols in strips(half, 256):
            m_ref[:, cols] = a_ref[:, cols] + add_up(l_ref, cols)
            far = slice(cols.start + half, cols.stop + half)
            t_ref[:, cols] = a_ref[:, far] + add_up(l_ref, far)

    return call(body, [((eight, half), f32)] * 2, landed, added)


def activate(landed):
    count, rows, deep = landed.shape

    def body(l_ref, p_ref, c_ref):
        for cols in strips(deep, 128):
            pre = add_up(l_ref, cols).astype(bf16)
            p_ref[:, cols] = pre
            value = gelu_parts(pre.astype(f32))[0].astype(bf16)
            for k in range(count):
                c_ref[k, :, cols] = value

    return call(body, [((rows, deep), bf16), ((count, rows, deep), bf16)], landed)


def activate_and_back(landed):
    count, rows, deep = landed.shape[0], landed.shape[1], landed.shape[2] // 2

    def body(l_ref, c_ref):
        for cols in strips(deep, 128):
            far = slice(cols.start + deep, cols.stop + deep)
            pre = add_up(l_ref, cols).astype(bf16)
            value, slope = gelu_parts(pre.astype(f32))
            value = value.astype(bf16)
            back = add_up(l_ref, far).astype(bf16)
            inner = (back.astype(f32) * slope).astype(bf16)
            for k in range(count):
                c_ref[k, :, cols] = inner
                c_ref[k, :, far] = value

    return call(body, [(landed.shape, bf16)], landed)


def back_through(landed, pre):
    count, rows, deep = landed.shape

    def body(l_ref, p_ref, c_ref):
        for cols in strips(deep, 128):
            slope = gelu_parts(p_ref[:, cols].astype(f32))[1]
            back = add_up(l_ref, cols).astype(bf16)
            inner = (back.astype(f32) * slope).astype(bf16)
            for k in range(count):
                c_ref[k, :, cols] = inner

    return call(body, [((count, rows, deep), bf16)], landed, pre)


def swap(block):
    return lax.ppermute(block, "core", [(0, 1), (1, 0)])


def exchange(parts, axes):
    return lax.all_to_all(parts, axes, 0, 0, tiled=True)


def shards(start_latent, target_one, target_two, w_up, w_down):
    n_y = SIZES["y"]
    n_h = SIZES["x"] * SIZES["z"]
    rows, wide = start_latent.shape
    deep = w_up.shape[1]
    eight = rows // (2 * n_h)
    half = rows // 2
    quarter = half // n_y
    core = lax.axis_index("core")
    place = lax.axis_index("x") * SIZES["z"] + lax.axis_index("z")

    def halves(full):
        cut = full.reshape(n_h, 2, eight, wide)
        own = lax.dynamic_index_in_dim(cut, core, 1, keepdims=False)
        other = lax.dynamic_index_in_dim(cut, 1 - core, 1, keepdims=False)
        return own, other

    def own_rows(*terms):
        first = 2 * eight * place
        pair = sum(lax.dynamic_slice_in_dim(full, first, 2 * eight, 0) for full in terms)
        mine = lax.dynamic_slice_in_dim(pair, eight * core, eight, 0)
        theirs = lax.dynamic_slice_in_dim(pair, eight * (1 - core), eight, 0)
        return jnp.concatenate([mine, swap(theirs)], axis=1)

    def rounded_halves(full):
        own, other = halves(full)
        return own.astype(bf16).reshape(half, wide), other.astype(bf16).reshape(half, wide)

    def both_cores(own, other_part):
        return (own + swap(other_part.astype(bf16)).astype(f32)).astype(bf16)

    down_other = swap(w_down)

    start_own, start_other = rounded_halves(start_latent)
    pre_part = both_cores(dot(start_own, w_up), dot(start_other, w_up))
    pre_zero, act_zero = activate(exchange(pre_part.reshape(n_y, quarter, deep), "y"))
    act_zero = exchange(act_zero, "y").reshape(half, deep)

    part = widen(dot, act_zero, w_down, down_other)
    landed = exchange(part.reshape(n_h, eight, 2 * wide), HIDDEN)
    up_other = swap(w_up)
    two_own, two_other = rounded_halves(target_two)
    back_part = both_cores(dot_t(two_own, w_down), dot_t(two_other, w_down))
    start_rows = own_rows(start_latent)
    target_rows = own_rows(target_one, target_two)
    landed, up_other, back_part, start_rows, target_rows = lax.optimization_barrier(
        (landed, up_other, back_part, start_rows, target_rows)
    )
    latent_one, input_one = sum_and_copy(landed, start_rows)
    input_one = exchange(input_one, HIDDEN).reshape(half, 2 * wide)

    pre_part = narrow(dot, input_one, w_up, up_other)
    both = jnp.concatenate([pre_part.reshape(n_y, quarter, deep), back_part.reshape(n_y, quarter, deep)], axis=2)
    one = activate_and_back(exchange(both, "y"))
    one = exchange(one, "y").reshape(half, 2 * deep)

    part = widen(dot_t, one, w_up, up_other)
    landed = exchange(part.reshape(n_h, eight, 2 * wide), HIDDEN)
    one_other = swap(one)
    input_far = swap(input_one[:, wide:])
    act_zero_other = swap(act_zero)
    landed, one_other, input_far, act_zero_other = lax.optimization_barrier(
        (landed, one_other, input_far, act_zero_other)
    )
    grad_one, error_one = sum_and_copy(landed, target_rows)
    error_one = exchange(error_one, HIDDEN).reshape(half, 2 * wide)

    back_part = narrow(dot_t, error_one, w_down, down_other)
    inner_zero = back_through(exchange(back_part.reshape(n_y, quarter, deep), "y"), pre_zero)
    inner_zero = exchange(inner_zero, "y").reshape(half, deep)

    part = widen(dot_t, inner_zero, w_up, up_other)
    landed = exchange(part.reshape(n_h, eight, 2 * wide), HIDDEN)

    grad_down = t_dot(
        jnp.concatenate([act_zero, act_zero_other, one[:, deep:], one_other[:, deep:]], axis=0),
        jnp.concatenate([error_one[:, :wide], swap(error_one[:, wide:]), two_own, two_other], axis=0),
    )
    grad_up = t_dot(
        jnp.concatenate([start_own, start_other, input_one[:, :wide], input_far], axis=0),
        jnp.concatenate([inner_zero, swap(inner_zero), one[:, :deep], one_other[:, :deep]], axis=0),
    )
    landed, grad_up, grad_down = lax.optimization_barrier((landed, grad_up, grad_down))

    mine, theirs = sum_last(landed, grad_one)
    theirs = swap(theirs)
    grad_start = jnp.where(
        core == 0, jnp.concatenate([mine, theirs], axis=0), jnp.concatenate([theirs, mine], axis=0)
    )
    return (grad_start, grad_up, grad_down)


def solution(mesh):
    fine = Mesh(mesh.devices.reshape(tuple(SIZES.values())), tuple(SIZES))
    width, hidden = ("y", "core"), HIDDEN
    return jax.shard_map(
        shards,
        mesh=fine,
        in_specs=(
            P(None, width),
            P(None, width),
            P(None, width),
            P(width, hidden),
            P(hidden, width),
        ),
        out_specs=(P(hidden, width), P(width, hidden), P(hidden, width)),
        check_vma=False,
    )
```

```python
import functools
import math

import jax
import jax.numpy as jnp
from jax import lax
from jax.experimental import pallas as pl
from jax.experimental.pallas import tpu as pltpu
from jax.sharding import Mesh, PartitionSpec as P

gelu_scale = math.sqrt(2.0 / math.pi)
cubic_coef = 0.044715
f32 = jnp.float32
bf16 = jnp.bfloat16
SIZES = {"y": 4, "core": 2, "x": 4, "z": 8}
HIDDEN = ("x", "z")
STRIP = 64


def gelu_parts(preact):
    inner = gelu_scale * (preact + cubic_coef * preact * preact * preact)
    tangent = jnp.tanh(inner)
    value_out = 0.5 * preact * (1.0 + tangent)
    slope_out = 0.5 * (1.0 + tangent) + 0.5 * preact * (1.0 - tangent * tangent) * gelu_scale * (
        1.0 + 3.0 * cubic_coef * preact * preact
    )
    return (value_out, slope_out)


def dot(a, b):
    return jnp.dot(a, b, preferred_element_type=f32)


def dot_t(a, b):
    return lax.dot_general(a, b, (((1,), (1,)), ((), ())), preferred_element_type=f32)


def t_dot(a, b):
    return lax.dot_general(a, b, (((0,), (0,)), ((), ())), preferred_element_type=f32)


def call(body, outs, *operands, flops=0):
    size = sum(math.prod(o.shape) * o.dtype.itemsize for o in operands)
    size += sum(math.prod(s) * jnp.dtype(t).itemsize for s, t in outs)
    got = pl.pallas_call(
        body,
        out_shape=[jax.ShapeDtypeStruct(s, t) for s, t in outs],
        in_specs=[pl.BlockSpec(memory_space=pltpu.VMEM)] * len(operands),
        out_specs=[pl.BlockSpec(memory_space=pltpu.VMEM)] * len(outs),
        cost_estimate=pl.CostEstimate(flops=flops, bytes_accessed=size, transcendentals=0),
        compiler_params=pltpu.CompilerParams(vmem_limit_bytes=24 * 2**20),
    )(*operands)
    return got[0] if len(outs) == 1 else got


def widen(product, rows_deep, own_block, other_block, by_rows):
    rows, wide = rows_deep.shape[0], own_block.shape[0]
    cut = wide // 2

    def body(x_ref, a_ref, b_ref, o_ref, held, sems):
        copies = []
        for part in range(4):
            block, first = (a_ref, b_ref)[part // 2], (part % 2) * cut
            piece = block[first : first + cut, :] if by_rows else block[:, first : first + cut]
            held[part] = product(x_ref[:, :wide], piece).astype(bf16)
            copies.append(
                pltpu.make_async_copy(held.at[part], o_ref.at[:, pl.ds(part * cut, cut)], sems.at[part])
            )
            copies[-1].start()
        for copy in copies:
            copy.wait()

    size = 2 * (rows_deep.size + 2 * own_block.size + 2 * rows * wide)
    return pl.pallas_call(
        body,
        out_shape=pltpu.HBM((rows, 2 * wide), bf16),
        in_specs=[pl.BlockSpec(memory_space=pltpu.VMEM)] * 3,
        out_specs=pl.BlockSpec(memory_space=pltpu.HBM),
        scratch_shapes=[pltpu.VMEM((4, rows, cut), bf16), pltpu.SemaphoreType.DMA((4,))],
        cost_estimate=pl.CostEstimate(flops=4 * rows * wide * wide, bytes_accessed=size, transcendentals=0),
        compiler_params=pltpu.CompilerParams(vmem_limit_bytes=24 * 2**20),
    )(rows_deep, own_block, other_block)


def narrow(product, rows_wide, own_block, other_block):
    rows, wide = rows_wide.shape[0], rows_wide.shape[1] // 2

    def body(x_ref, a_ref, b_ref, o_ref):
        total = product(x_ref[:, :wide], a_ref[...]) + product(x_ref[:, wide:], b_ref[...])
        o_ref[...] = total.astype(bf16)

    return call(
        body, [((rows, wide), bf16)], rows_wide, own_block, other_block, flops=4 * rows * wide * wide
    )


def add_up(ref, columns):
    total = ref[0, :, columns].astype(f32)
    for k in range(1, ref.shape[0]):
        total = total + ref[k, :, columns].astype(f32)
    return total


def strips(width, step):
    return [slice(first, first + step) for first in range(0, width, step)]


def sum_and_copy(landed, added):
    count, eight, wide = landed.shape

    def body(l_ref, a_ref, s_ref, c_ref):
        for cols in strips(wide, 256):
            total = a_ref[:, cols] + add_up(l_ref, cols)
            s_ref[:, cols] = total
            rounded = total.astype(bf16)
            for k in range(count):
                c_ref[k, :, cols] = rounded

    return call(body, [((eight, wide), f32), ((count, eight, wide), bf16)], landed, added)


def sum_last(landed, added):
    count, eight, wide = landed.shape
    half = wide // 2

    def body(l_ref, a_ref, m_ref, t_ref):
        for cols in strips(half, 256):
            m_ref[:, cols] = a_ref[:, cols] + add_up(l_ref, cols)
            far = slice(cols.start + half, cols.stop + half)
            t_ref[:, cols] = a_ref[:, far] + add_up(l_ref, far)

    return call(body, [((eight, half), f32)] * 2, landed, added)


def activate(landed):
    count, rows, deep = landed.shape

    def body(l_ref, p_ref, c_ref):
        for cols in strips(deep, 128):
            pre = add_up(l_ref, cols).astype(bf16)
            p_ref[:, cols] = pre
            value = gelu_parts(pre.astype(f32))[0].astype(bf16)
            for k in range(count):
                c_ref[k, :, cols] = value

    return call(body, [((rows, deep), bf16), ((count, rows, deep), bf16)], landed)


def activate_and_back(landed):
    count, rows, deep = landed.shape[0], landed.shape[1], landed.shape[2] // 2

    def body(l_ref, c_ref):
        for cols in strips(deep, 128):
            far = slice(cols.start + deep, cols.stop + deep)
            pre = add_up(l_ref, cols).astype(bf16)
            value, slope = gelu_parts(pre.astype(f32))
            value = value.astype(bf16)
            back = add_up(l_ref, far).astype(bf16)
            inner = (back.astype(f32) * slope).astype(bf16)
            for k in range(count):
                c_ref[k, :, cols] = inner
                c_ref[k, :, far] = value

    return call(body, [(landed.shape, bf16)], landed)


def back_through(landed, pre):
    count, rows, deep = landed.shape

    def body(l_ref, p_ref, c_ref):
        for cols in strips(deep, 128):
            slope = gelu_parts(p_ref[:, cols].astype(f32))[1]
            back = add_up(l_ref, cols).astype(bf16)
            inner = (back.astype(f32) * slope).astype(bf16)
            for k in range(count):
                c_ref[k, :, cols] = inner

    return call(body, [((count, rows, deep), bf16)], landed, pre)


def swap(block):
    return lax.ppermute(block, "core", [(0, 1), (1, 0)])


def swap_parts(block):
    step = block.shape[0] // 2
    return jnp.concatenate([swap(block[first : first + step]) for first in range(0, block.shape[0], step)], axis=0)


def exchange(parts, axes):
    return lax.all_to_all(parts, axes, 0, 0, tiled=True)


def shards(start_latent, target_one, target_two, w_up, w_down):
    n_y = SIZES["y"]
    n_h = SIZES["x"] * SIZES["z"]
    rows, wide = start_latent.shape
    deep = w_up.shape[1]
    eight = rows // (2 * n_h)
    half = rows // 2
    quarter = half // n_y
    core = lax.axis_index("core")
    place = lax.axis_index("x") * SIZES["z"] + lax.axis_index("z")

    def halves(full):
        cut = full.reshape(n_h, 2, eight, wide)
        own = lax.dynamic_index_in_dim(cut, core, 1, keepdims=False)
        other = lax.dynamic_index_in_dim(cut, 1 - core, 1, keepdims=False)
        return own, other

    def own_rows(*terms):
        first = 2 * eight * place
        pair = sum(lax.dynamic_slice_in_dim(full, first, 2 * eight, 0) for full in terms)
        mine = lax.dynamic_slice_in_dim(pair, eight * core, eight, 0)
        theirs = lax.dynamic_slice_in_dim(pair, eight * (1 - core), eight, 0)
        return jnp.concatenate([mine, swap(theirs)], axis=1)

    def rounded_halves(full):
        own, other = halves(full)
        return own.astype(bf16).reshape(half, wide), other.astype(bf16).reshape(half, wide)

    def both_cores(own, other_part):
        return (own + swap(other_part.astype(bf16)).astype(f32)).astype(bf16)

    down_other = swap(w_down)
    up_other = swap(w_up)

    start_own, start_other = rounded_halves(start_latent)
    pre_part = both_cores(dot(start_own, w_up), dot(start_other, w_up))
    pre_zero, act_zero = activate(exchange(pre_part.reshape(n_y, quarter, deep), "y"))
    act_zero, up_other = lax.optimization_barrier((exchange(act_zero, "y").reshape(half, deep), up_other))

    part = widen(dot, act_zero, w_down, down_other, False)
    landed = exchange(part.reshape(n_h, eight, 2 * wide), HIDDEN)
    two_own, two_other = rounded_halves(target_two)
    two_far = swap(two_other)
    start_far = swap(start_other)
    back_part = (dot_t(two_own, w_down) + dot_t(two_far, down_other)).astype(bf16)
    start_rows = own_rows(start_latent)
    target_rows = own_rows(target_one, target_two)
    landed, back_part, start_rows, target_rows, start_far = lax.optimization_barrier(
        (landed, back_part, start_rows, target_rows, start_far)
    )
    latent_one, input_one = sum_and_copy(landed, start_rows)
    input_one = exchange(input_one, HIDDEN).reshape(half, 2 * wide)

    pre_part = narrow(dot, input_one, w_up, up_other)
    both = jnp.concatenate([pre_part.reshape(n_y, quarter, deep), back_part.reshape(n_y, quarter, deep)], axis=2)
    one = activate_and_back(exchange(both, "y"))
    one = exchange(one, "y").reshape(half, 2 * deep)

    part = widen(dot_t, one, w_up, up_other, True)
    landed = exchange(part.reshape(n_h, eight, 2 * wide), HIDDEN)
    grad_one, error_one = sum_and_copy(landed, target_rows)
    error_one = exchange(error_one, HIDDEN).reshape(half, 2 * wide)

    back_part = narrow(dot_t, error_one, w_down, down_other)
    inner_zero = back_through(exchange(back_part.reshape(n_y, quarter, deep), "y"), pre_zero)
    inner_zero = exchange(inner_zero, "y").reshape(half, deep)

    part = widen(dot_t, inner_zero, w_up, up_other, True)
    part, inner_zero, error_one, one, act_zero, input_one = lax.optimization_barrier(
        (part, inner_zero, error_one, one, act_zero, input_one)
    )
    landed = exchange(part.reshape(n_h, eight, 2 * wide), HIDDEN)

    inner_both = jnp.concatenate([inner_zero, one[:, :deep]], axis=0)
    act_both = jnp.concatenate([act_zero, one[:, deep:]], axis=0)
    up_far = t_dot(jnp.concatenate([start_far, input_one[:, wide:]], axis=0), inner_both).astype(bf16)
    down_far = t_dot(act_both, jnp.concatenate([error_one[:, wide:], two_far], axis=0)).astype(bf16)
    grad_up = t_dot(jnp.concatenate([start_own, input_one[:, :wide]], axis=0), inner_both) + swap_parts(up_far)
    grad_down = t_dot(act_both, jnp.concatenate([error_one[:, :wide], two_own], axis=0)) + swap_parts(down_far)
    landed, grad_up, grad_down = lax.optimization_barrier((landed, grad_up, grad_down))

    mine, theirs = sum_last(landed, grad_one)
    theirs = swap(theirs)
    grad_start = jnp.where(
        core == 0, jnp.concatenate([mine, theirs], axis=0), jnp.concatenate([theirs, mine], axis=0)
    )
    return (grad_start, grad_up, grad_down)


def solution(mesh):
    fine = Mesh(mesh.devices.reshape(tuple(SIZES.values())), tuple(SIZES))
    width, hidden = ("y", "core"), HIDDEN
    return jax.shard_map(
        shards,
        mesh=fine,
        in_specs=(
            P(None, width),
            P(None, width),
            P(None, width),
            P(width, hidden),
            P(hidden, width),
        ),
        out_specs=(P(hidden, width), P(width, hidden), P(hidden, width)),
        check_vma=False,
    )
```

```python
import functools
import math

import jax
import jax.numpy as jnp
from jax import lax
from jax.experimental import pallas as pl
from jax.experimental.pallas import tpu as pltpu
from jax.sharding import Mesh, PartitionSpec as P

gelu_scale = math.sqrt(2.0 / math.pi)
cubic_coef = 0.044715
f32 = jnp.float32
bf16 = jnp.bfloat16
SIZES = {"y": 4, "core": 2, "x": 4, "z": 8}
HIDDEN = ("x", "z")
STRIP = 64


def gelu_parts(preact):
    inner = gelu_scale * (preact + cubic_coef * preact * preact * preact)
    tangent = jnp.tanh(inner)
    value_out = 0.5 * preact * (1.0 + tangent)
    slope_out = 0.5 * (1.0 + tangent) + 0.5 * preact * (1.0 - tangent * tangent) * gelu_scale * (
        1.0 + 3.0 * cubic_coef * preact * preact
    )
    return (value_out, slope_out)


def dot(a, b):
    return jnp.dot(a, b, preferred_element_type=f32)


def dot_t(a, b):
    return lax.dot_general(a, b, (((1,), (1,)), ((), ())), preferred_element_type=f32)


def t_dot(a, b):
    return lax.dot_general(a, b, (((0,), (0,)), ((), ())), preferred_element_type=f32)


def call(body, outs, *operands, flops=0):
    size = sum(math.prod(o.shape) * o.dtype.itemsize for o in operands)
    size += sum(math.prod(s) * jnp.dtype(t).itemsize for s, t in outs)
    got = pl.pallas_call(
        body,
        out_shape=[jax.ShapeDtypeStruct(s, t) for s, t in outs],
        in_specs=[pl.BlockSpec(memory_space=pltpu.VMEM)] * len(operands),
        out_specs=[pl.BlockSpec(memory_space=pltpu.VMEM)] * len(outs),
        cost_estimate=pl.CostEstimate(flops=flops, bytes_accessed=size, transcendentals=0),
        compiler_params=pltpu.CompilerParams(vmem_limit_bytes=24 * 2**20),
    )(*operands)
    return got[0] if len(outs) == 1 else got


def widen(product, rows_deep, own_block, other_block, by_rows):
    rows, wide = rows_deep.shape[0], own_block.shape[0]
    cut = wide // 2

    def body(x_ref, a_ref, b_ref, o_ref, held, sems):
        copies = []
        for part in range(4):
            block, first = (a_ref, b_ref)[part // 2], (part % 2) * cut
            piece = block[first : first + cut, :] if by_rows else block[:, first : first + cut]
            held[part] = product(x_ref[:, :wide], piece).astype(bf16)
            copies.append(
                pltpu.make_async_copy(held.at[part], o_ref.at[:, pl.ds(part * cut, cut)], sems.at[part])
            )
            copies[-1].start()
        for copy in copies:
            copy.wait()

    size = 2 * (rows_deep.size + 2 * own_block.size + 2 * rows * wide)
    return pl.pallas_call(
        body,
        out_shape=pltpu.HBM((rows, 2 * wide), bf16),
        in_specs=[pl.BlockSpec(memory_space=pltpu.VMEM)] * 3,
        out_specs=pl.BlockSpec(memory_space=pltpu.HBM),
        scratch_shapes=[pltpu.VMEM((4, rows, cut), bf16), pltpu.SemaphoreType.DMA((4,))],
        cost_estimate=pl.CostEstimate(flops=4 * rows * wide * wide, bytes_accessed=size, transcendentals=0),
        compiler_params=pltpu.CompilerParams(vmem_limit_bytes=24 * 2**20),
    )(rows_deep, own_block, other_block)


def widen_near(product, rows_deep, own_block, other_block):
    rows, wide = rows_deep.shape[0], own_block.shape[0]

    def body(x_ref, a_ref, b_ref, o_ref):
        o_ref[:, :wide] = product(x_ref[:, :wide], a_ref[...]).astype(bf16)
        o_ref[:, wide:] = product(x_ref[:, :wide], b_ref[...]).astype(bf16)

    return call(
        body, [((rows, 2 * wide), bf16)], rows_deep, own_block, other_block, flops=4 * rows * wide * wide
    )


def narrow(product, rows_wide, own_block, other_block, beside=None):
    rows, wide = rows_wide.shape[0], rows_wide.shape[1] // 2
    more = [] if beside is None else [beside]

    def body(x_ref, a_ref, b_ref, *refs):
        total = product(x_ref[:, :wide], a_ref[...]) + product(x_ref[:, wide:], b_ref[...])
        refs[-1][:, :wide] = total.astype(bf16)
        if more:
            refs[-1][:, wide:] = refs[0][...]

    out = ((rows, wide * (1 + len(more))), bf16)
    return call(body, [out], rows_wide, own_block, other_block, *more, flops=4 * rows * wide * wide)


def add_up(ref, columns):
    total = ref[0, :, columns].astype(f32)
    for k in range(1, ref.shape[0]):
        total = total + ref[k, :, columns].astype(f32)
    return total


def strips(width, step):
    return [slice(first, first + step) for first in range(0, width, step)]


def sum_and_copy(landed, added):
    count, eight, wide = landed.shape

    def body(l_ref, a_ref, s_ref, c_ref):
        for cols in strips(wide, 256):
            total = a_ref[:, cols] + add_up(l_ref, cols)
            s_ref[:, cols] = total
            rounded = total.astype(bf16)
            for k in range(count):
                c_ref[k, :, cols] = rounded

    return call(body, [((eight, wide), f32), ((count, eight, wide), bf16)], landed, added)


def sum_last(landed, added):
    count, eight, wide = landed.shape
    half = wide // 2

    def body(l_ref, a_ref, m_ref, t_ref):
        for cols in strips(half, 256):
            m_ref[:, cols] = a_ref[:, cols] + add_up(l_ref, cols)
            far = slice(cols.start + half, cols.stop + half)
            t_ref[:, cols] = a_ref[:, far] + add_up(l_ref, far)

    return call(body, [((eight, half), f32)] * 2, landed, added)


def activate(landed):
    count, rows, deep = landed.shape

    def body(l_ref, p_ref, c_ref):
        for cols in strips(deep, 128):
            pre = add_up(l_ref, cols).astype(bf16)
            p_ref[:, cols] = pre
            value = gelu_parts(pre.astype(f32))[0].astype(bf16)
            for k in range(count):
                c_ref[k, :, cols] = value

    return call(body, [((rows, deep), bf16), ((count, rows, deep), bf16)], landed)


def activate_and_back(landed):
    count, rows, deep = landed.shape[0], landed.shape[1], landed.shape[2] // 2

    def body(l_ref, c_ref):
        for cols in strips(deep, 128):
            far = slice(cols.start + deep, cols.stop + deep)
            pre = add_up(l_ref, cols).astype(bf16)
            value, slope = gelu_parts(pre.astype(f32))
            value = value.astype(bf16)
            back = add_up(l_ref, far).astype(bf16)
            inner = (back.astype(f32) * slope).astype(bf16)
            for k in range(count):
                c_ref[k, :, cols] = inner
                c_ref[k, :, far] = value

    return call(body, [(landed.shape, bf16)], landed)


def back_through(landed, pre):
    count, rows, deep = landed.shape

    def body(l_ref, p_ref, c_ref):
        for cols in strips(deep, 128):
            slope = gelu_parts(p_ref[:, cols].astype(f32))[1]
            back = add_up(l_ref, cols).astype(bf16)
            inner = (back.astype(f32) * slope).astype(bf16)
            for k in range(count):
                c_ref[k, :, cols] = inner

    return call(body, [((count, rows, deep), bf16)], landed, pre)


def swap(block):
    return lax.ppermute(block, "core", [(0, 1), (1, 0)])


def swap_parts(block):
    step = block.shape[0] // 2
    return jnp.concatenate([swap(block[first : first + step]) for first in range(0, block.shape[0], step)], axis=0)


def exchange(parts, axes):
    return lax.all_to_all(parts, axes, 0, 0, tiled=True)


def shards(start_latent, target_one, target_two, w_up, w_down):
    n_y = SIZES["y"]
    n_h = SIZES["x"] * SIZES["z"]
    rows, wide = start_latent.shape
    deep = w_up.shape[1]
    eight = rows // (2 * n_h)
    half = rows // 2
    quarter = half // n_y
    core = lax.axis_index("core")
    place = lax.axis_index("x") * SIZES["z"] + lax.axis_index("z")

    def halves(full):
        cut = full.reshape(n_h, 2, eight, wide)
        own = lax.dynamic_index_in_dim(cut, core, 1, keepdims=False)
        other = lax.dynamic_index_in_dim(cut, 1 - core, 1, keepdims=False)
        return own, other

    def own_rows(*terms):
        first = 2 * eight * place
        pair = sum(lax.dynamic_slice_in_dim(full, first, 2 * eight, 0) for full in terms)
        mine = lax.dynamic_slice_in_dim(pair, eight * core, eight, 0)
        theirs = lax.dynamic_slice_in_dim(pair, eight * (1 - core), eight, 0)
        return jnp.concatenate([mine, swap(theirs)], axis=1)

    def rounded_halves(full):
        own, other = halves(full)
        return own.astype(bf16).reshape(half, wide), other.astype(bf16).reshape(half, wide)

    def both_cores(own, other_part):
        return (own + swap(other_part.astype(bf16)).astype(f32)).astype(bf16)

    down_other = swap(w_down)
    up_other = swap(w_up)

    start_own, start_other = rounded_halves(start_latent)
    pre_part = both_cores(dot(start_own, w_up), dot(start_other, w_up))
    pre_zero, act_zero = activate(exchange(pre_part.reshape(n_y, quarter, deep), "y"))
    act_zero, up_other = lax.optimization_barrier((exchange(act_zero, "y").reshape(half, deep), up_other))

    part = widen(dot, act_zero, w_down, down_other, False)
    landed = exchange(part.reshape(n_h, eight, 2 * wide), HIDDEN)
    two_own, two_other = rounded_halves(target_two)
    two_far = swap(two_other)
    start_far = swap(start_other)
    back_part = (dot_t(two_own, w_down) + dot_t(two_far, down_other)).astype(bf16)
    start_rows = own_rows(start_latent)
    target_rows = own_rows(target_one, target_two)
    landed, back_part, start_rows, target_rows, start_far = lax.optimization_barrier(
        (landed, back_part, start_rows, target_rows, start_far)
    )
    latent_one, input_one = sum_and_copy(landed, start_rows)
    input_one = exchange(input_one, HIDDEN).reshape(half, 2 * wide)

    both = narrow(dot, input_one, w_up, up_other, back_part).reshape(n_y, quarter, 2 * deep)
    one = activate_and_back(exchange(both, "y"))
    one = exchange(one, "y").reshape(half, 2 * deep)

    part = widen_near(dot_t, one, w_up, up_other)
    landed = exchange(part.reshape(n_h, eight, 2 * wide), HIDDEN)
    grad_one, error_one = sum_and_copy(landed, target_rows)
    error_one = exchange(error_one, HIDDEN).reshape(half, 2 * wide)

    back_part = narrow(dot_t, error_one, w_down, down_other)
    inner_zero = back_through(exchange(back_part.reshape(n_y, quarter, deep), "y"), pre_zero)
    inner_zero = exchange(inner_zero, "y").reshape(half, deep)

    part = widen(dot_t, inner_zero, w_up, up_other, True)
    part, inner_zero, error_one, one, act_zero, input_one = lax.optimization_barrier(
        (part, inner_zero, error_one, one, act_zero, input_one)
    )
    landed = exchange(part.reshape(n_h, eight, 2 * wide), HIDDEN)

    inner_both = jnp.concatenate([inner_zero, one[:, :deep]], axis=0)
    act_both = jnp.concatenate([act_zero, one[:, deep:]], axis=0)
    up_far = t_dot(jnp.concatenate([start_far, input_one[:, wide:]], axis=0), inner_both).astype(bf16)
    down_far = t_dot(act_both, jnp.concatenate([error_one[:, wide:], two_far], axis=0)).astype(bf16)
    grad_up = t_dot(jnp.concatenate([start_own, input_one[:, :wide]], axis=0), inner_both) + swap_parts(up_far)
    grad_down = t_dot(act_both, jnp.concatenate([error_one[:, :wide], two_own], axis=0)) + swap_parts(down_far)
    landed, grad_up, grad_down = lax.optimization_barrier((landed, grad_up, grad_down))

    mine, theirs = sum_last(landed, grad_one)
    theirs = swap(theirs)
    grad_start = jnp.where(
        core == 0, jnp.concatenate([mine, theirs], axis=0), jnp.concatenate([theirs, mine], axis=0)
    )
    return (grad_start, grad_up, grad_down)


def solution(mesh):
    fine = Mesh(mesh.devices.reshape(tuple(SIZES.values())), tuple(SIZES))
    width, hidden = ("y", "core"), HIDDEN
    return jax.shard_map(
        shards,
        mesh=fine,
        in_specs=(
            P(None, width),
            P(None, width),
            P(None, width),
            P(width, hidden),
            P(hidden, width),
        ),
        out_specs=(P(hidden, width), P(width, hidden), P(hidden, width)),
        check_vma=False,
    )
```

```python
import functools
import math

import jax
import jax.numpy as jnp
from jax import lax
from jax.experimental import pallas as pl
from jax.experimental.pallas import tpu as pltpu
from jax.sharding import Mesh, PartitionSpec as P

gelu_scale = math.sqrt(2.0 / math.pi)
cubic_coef = 0.044715
f32 = jnp.float32
bf16 = jnp.bfloat16
SIZES = {"y": 4, "core": 2, "x": 4, "z": 8}
HIDDEN = ("x", "z")
STRIP = 64


def gelu_parts(preact):
    inner = gelu_scale * (preact + cubic_coef * preact * preact * preact)
    tangent = jnp.tanh(inner)
    value_out = 0.5 * preact * (1.0 + tangent)
    slope_out = 0.5 * (1.0 + tangent) + 0.5 * preact * (1.0 - tangent * tangent) * gelu_scale * (
        1.0 + 3.0 * cubic_coef * preact * preact
    )
    return (value_out, slope_out)


def dot(a, b):
    return jnp.dot(a, b, preferred_element_type=f32)


def dot_t(a, b):
    return lax.dot_general(a, b, (((1,), (1,)), ((), ())), preferred_element_type=f32)


def t_dot(a, b):
    return lax.dot_general(a, b, (((0,), (0,)), ((), ())), preferred_element_type=f32)


def call(body, outs, *operands, flops=0):
    size = sum(math.prod(o.shape) * o.dtype.itemsize for o in operands)
    size += sum(math.prod(s) * jnp.dtype(t).itemsize for s, t in outs)
    got = pl.pallas_call(
        body,
        out_shape=[jax.ShapeDtypeStruct(s, t) for s, t in outs],
        in_specs=[pl.BlockSpec(memory_space=pltpu.VMEM)] * len(operands),
        out_specs=[pl.BlockSpec(memory_space=pltpu.VMEM)] * len(outs),
        cost_estimate=pl.CostEstimate(flops=flops, bytes_accessed=size, transcendentals=0),
        compiler_params=pltpu.CompilerParams(vmem_limit_bytes=24 * 2**20),
    )(*operands)
    return got[0] if len(outs) == 1 else got


def widen(product, rows_deep, own_block, other_block, by_rows):
    rows, wide = rows_deep.shape[0], own_block.shape[0]
    cut = wide // 2

    def body(x_ref, a_ref, b_ref, o_ref, held, sems):
        copies = []
        for part in range(4):
            block, first = (a_ref, b_ref)[part // 2], (part % 2) * cut
            piece = block[first : first + cut, :] if by_rows else block[:, first : first + cut]
            held[part] = product(x_ref[:, :wide], piece).astype(bf16)
            copies.append(
                pltpu.make_async_copy(held.at[part], o_ref.at[:, pl.ds(part * cut, cut)], sems.at[part])
            )
            copies[-1].start()
        for copy in copies:
            copy.wait()

    size = 2 * (rows_deep.size + 2 * own_block.size + 2 * rows * wide)
    return pl.pallas_call(
        body,
        out_shape=pltpu.HBM((rows, 2 * wide), bf16),
        in_specs=[pl.BlockSpec(memory_space=pltpu.VMEM)] * 3,
        out_specs=pl.BlockSpec(memory_space=pltpu.HBM),
        scratch_shapes=[pltpu.VMEM((4, rows, cut), bf16), pltpu.SemaphoreType.DMA((4,))],
        cost_estimate=pl.CostEstimate(flops=4 * rows * wide * wide, bytes_accessed=size, transcendentals=0),
        compiler_params=pltpu.CompilerParams(vmem_limit_bytes=24 * 2**20),
    )(rows_deep, own_block, other_block)


def widen_near(product, rows_deep, own_block, other_block):
    rows, wide = rows_deep.shape[0], own_block.shape[0]

    def body(x_ref, a_ref, b_ref, o_ref):
        o_ref[:, :wide] = product(x_ref[:, :wide], a_ref[...]).astype(bf16)
        o_ref[:, wide:] = product(x_ref[:, :wide], b_ref[...]).astype(bf16)

    return call(
        body, [((rows, 2 * wide), bf16)], rows_deep, own_block, other_block, flops=4 * rows * wide * wide
    )


def narrow(product, rows_wide, own_block, other_block, beside=None):
    rows, wide = rows_wide.shape[0], rows_wide.shape[1] // 2
    more = [] if beside is None else [beside]

    def body(x_ref, a_ref, b_ref, *refs):
        total = product(x_ref[:, :wide], a_ref[...]) + product(x_ref[:, wide:], b_ref[...])
        refs[-1][:, :wide] = total.astype(bf16)
        if more:
            refs[-1][:, wide:] = refs[0][...]

    out = ((rows, wide * (1 + len(more))), bf16)
    return call(body, [out], rows_wide, own_block, other_block, *more, flops=4 * rows * wide * wide)


def add_up(ref, columns):
    total = ref[0, :, columns].astype(f32)
    for k in range(1, ref.shape[0]):
        total = total + ref[k, :, columns].astype(f32)
    return total


def strips(width, step):
    return [slice(first, first + step) for first in range(0, width, step)]


def sum_and_copy(landed, added):
    count, eight, wide = landed.shape

    def body(l_ref, a_ref, s_ref, c_ref):
        for cols in strips(wide, 256):
            total = a_ref[:, cols] + add_up(l_ref, cols)
            s_ref[:, cols] = total
            rounded = total.astype(bf16)
            for k in range(count):
                c_ref[k, :, cols] = rounded

    return call(body, [((eight, wide), f32), ((count, eight, wide), bf16)], landed, added)


def sum_half(landed, added, first):
    count, eight, wide = landed.shape
    half = wide // 2

    def body(l_ref, a_ref, o_ref):
        for cols in strips(half, 256):
            taken = slice(cols.start + first, cols.stop + first)
            o_ref[:, cols] = a_ref[:, taken] + add_up(l_ref, taken)

    return call(body, [((eight, half), f32)], landed, added)


def activate(landed):
    count, rows, deep = landed.shape

    def body(l_ref, p_ref, c_ref):
        for cols in strips(deep, 128):
            pre = add_up(l_ref, cols).astype(bf16)
            p_ref[:, cols] = pre
            value = gelu_parts(pre.astype(f32))[0].astype(bf16)
            for k in range(count):
                c_ref[k, :, cols] = value

    return call(body, [((rows, deep), bf16), ((count, rows, deep), bf16)], landed)


def activate_and_back(landed):
    count, rows, deep = landed.shape[0], landed.shape[1], landed.shape[2] // 2

    def body(l_ref, c_ref):
        for cols in strips(deep, 128):
            far = slice(cols.start + deep, cols.stop + deep)
            pre = add_up(l_ref, cols).astype(bf16)
            value, slope = gelu_parts(pre.astype(f32))
            value = value.astype(bf16)
            back = add_up(l_ref, far).astype(bf16)
            inner = (back.astype(f32) * slope).astype(bf16)
            for k in range(count):
                c_ref[k, :, cols] = inner
                c_ref[k, :, far] = value

    return call(body, [(landed.shape, bf16)], landed)


def back_through(landed, pre):
    count, rows, deep = landed.shape

    def body(l_ref, p_ref, c_ref):
        for cols in strips(deep, 128):
            slope = gelu_parts(p_ref[:, cols].astype(f32))[1]
            back = add_up(l_ref, cols).astype(bf16)
            inner = (back.astype(f32) * slope).astype(bf16)
            for k in range(count):
                c_ref[k, :, cols] = inner

    return call(body, [((count, rows, deep), bf16)], landed, pre)


def swap(block):
    return lax.ppermute(block, "core", [(0, 1), (1, 0)])


def swap_parts(block):
    step = block.shape[0] // 2
    return jnp.concatenate([swap(block[first : first + step]) for first in range(0, block.shape[0], step)], axis=0)


def exchange(parts, axes):
    return lax.all_to_all(parts, axes, 0, 0, tiled=True)


def shards(start_latent, target_one, target_two, w_up, w_down):
    n_y = SIZES["y"]
    n_h = SIZES["x"] * SIZES["z"]
    rows, wide = start_latent.shape
    deep = w_up.shape[1]
    eight = rows // (2 * n_h)
    half = rows // 2
    quarter = half // n_y
    core = lax.axis_index("core")
    place = lax.axis_index("x") * SIZES["z"] + lax.axis_index("z")

    def halves(full):
        cut = full.reshape(n_h, 2, eight, wide)
        own = lax.dynamic_index_in_dim(cut, core, 1, keepdims=False)
        other = lax.dynamic_index_in_dim(cut, 1 - core, 1, keepdims=False)
        return own, other

    def own_rows(*terms):
        first = 2 * eight * place
        pair = sum(lax.dynamic_slice_in_dim(full, first, 2 * eight, 0) for full in terms)
        mine = lax.dynamic_slice_in_dim(pair, eight * core, eight, 0)
        theirs = lax.dynamic_slice_in_dim(pair, eight * (1 - core), eight, 0)
        return jnp.concatenate([mine, swap(theirs)], axis=1)

    def rounded_halves(full):
        own, other = halves(full)
        return own.astype(bf16).reshape(half, wide), other.astype(bf16).reshape(half, wide)

    def both_cores(own, other_part):
        return (own + swap(other_part.astype(bf16)).astype(f32)).astype(bf16)

    down_other = swap(w_down)
    up_other = swap(w_up)

    start_own, start_other = rounded_halves(start_latent)
    pre_part = both_cores(dot(start_own, w_up), dot(start_other, w_up))
    pre_zero, act_zero = activate(exchange(pre_part.reshape(n_y, quarter, deep), "y"))
    act_zero, up_other = lax.optimization_barrier((exchange(act_zero, "y").reshape(half, deep), up_other))

    part = widen(dot, act_zero, w_down, down_other, False)
    landed = exchange(part.reshape(n_h, eight, 2 * wide), HIDDEN)
    two_own, two_other = rounded_halves(target_two)
    two_far = swap(two_other)
    start_far = swap(start_other)
    back_part = (dot_t(two_own, w_down) + dot_t(two_far, down_other)).astype(bf16)
    start_rows = own_rows(start_latent)
    target_rows = own_rows(target_one, target_two)
    landed, back_part, start_rows, target_rows, start_far = lax.optimization_barrier(
        (landed, back_part, start_rows, target_rows, start_far)
    )
    latent_one, input_one = sum_and_copy(landed, start_rows)
    input_one = exchange(input_one, HIDDEN).reshape(half, 2 * wide)

    both = narrow(dot, input_one, w_up, up_other, back_part).reshape(n_y, quarter, 2 * deep)
    one = activate_and_back(exchange(both, "y"))
    one = exchange(one, "y").reshape(half, 2 * deep)

    part = widen_near(dot_t, one, w_up, up_other)
    landed = exchange(part.reshape(n_h, eight, 2 * wide), HIDDEN)
    grad_one, error_one = sum_and_copy(landed, target_rows)
    error_one = exchange(error_one, HIDDEN).reshape(half, 2 * wide)

    back_part = narrow(dot_t, error_one, w_down, down_other)
    inner_zero = back_through(exchange(back_part.reshape(n_y, quarter, deep), "y"), pre_zero)
    inner_zero = exchange(inner_zero, "y").reshape(half, deep)

    part = widen(dot_t, inner_zero, w_up, up_other, True)
    part, inner_zero, error_one, one, act_zero, input_one = lax.optimization_barrier(
        (part, inner_zero, error_one, one, act_zero, input_one)
    )
    landed = exchange(part.reshape(n_h, eight, 2 * wide), HIDDEN)

    inner_both = jnp.concatenate([inner_zero, one[:, :deep]], axis=0)
    act_both = jnp.concatenate([act_zero, one[:, deep:]], axis=0)
    up_far = t_dot(jnp.concatenate([start_far, input_one[:, wide:]], axis=0), inner_both).astype(bf16)
    down_far = t_dot(act_both, jnp.concatenate([error_one[:, wide:], two_far], axis=0)).astype(bf16)
    grad_up = t_dot(jnp.concatenate([start_own, input_one[:, :wide]], axis=0), inner_both) + swap_parts(up_far)
    grad_down = t_dot(act_both, jnp.concatenate([error_one[:, :wide], two_own], axis=0)) + swap_parts(down_far)
    landed, grad_up, grad_down = lax.optimization_barrier((landed, grad_up, grad_down))

    theirs = swap(sum_half(landed, grad_one, wide))
    mine = sum_half(landed, grad_one, 0)
    grad_start = jnp.where(
        core == 0, jnp.concatenate([mine, theirs], axis=0), jnp.concatenate([theirs, mine], axis=0)
    )
    return (grad_start, grad_up, grad_down)


def solution(mesh):
    fine = Mesh(mesh.devices.reshape(tuple(SIZES.values())), tuple(SIZES))
    width, hidden = ("y", "core"), HIDDEN
    return jax.shard_map(
        shards,
        mesh=fine,
        in_specs=(
            P(None, width),
            P(None, width),
            P(None, width),
            P(width, hidden),
            P(hidden, width),
        ),
        out_specs=(P(hidden, width), P(width, hidden), P(hidden, width)),
        check_vma=False,
    )
```

```python
import functools
import math

import jax
import jax.numpy as jnp
from jax import lax
from jax.experimental import pallas as pl
from jax.experimental.pallas import tpu as pltpu
from jax.sharding import Mesh, PartitionSpec as P

gelu_scale = math.sqrt(2.0 / math.pi)
cubic_coef = 0.044715
f32 = jnp.float32
bf16 = jnp.bfloat16
SIZES = {"y": 4, "core": 2, "x": 4, "z": 8}
HIDDEN = ("x", "z")
STRIP = 64


def gelu_parts(preact):
    inner = gelu_scale * (preact + cubic_coef * preact * preact * preact)
    tangent = jnp.tanh(inner)
    value_out = 0.5 * preact * (1.0 + tangent)
    slope_out = 0.5 * (1.0 + tangent) + 0.5 * preact * (1.0 - tangent * tangent) * gelu_scale * (
        1.0 + 3.0 * cubic_coef * preact * preact
    )
    return (value_out, slope_out)


def dot(a, b):
    return jnp.dot(a, b, preferred_element_type=f32)


def dot_t(a, b):
    return lax.dot_general(a, b, (((1,), (1,)), ((), ())), preferred_element_type=f32)


def t_dot(a, b):
    return lax.dot_general(a, b, (((0,), (0,)), ((), ())), preferred_element_type=f32)


def call(body, outs, *operands, flops=0):
    size = sum(math.prod(o.shape) * o.dtype.itemsize for o in operands)
    size += sum(math.prod(s) * jnp.dtype(t).itemsize for s, t in outs)
    got = pl.pallas_call(
        body,
        out_shape=[jax.ShapeDtypeStruct(s, t) for s, t in outs],
        in_specs=[pl.BlockSpec(memory_space=pltpu.VMEM)] * len(operands),
        out_specs=[pl.BlockSpec(memory_space=pltpu.VMEM)] * len(outs),
        cost_estimate=pl.CostEstimate(flops=flops, bytes_accessed=size, transcendentals=0),
        compiler_params=pltpu.CompilerParams(vmem_limit_bytes=24 * 2**20),
    )(*operands)
    return got[0] if len(outs) == 1 else got


def widen(product, rows_deep, own_block, other_block, by_rows):
    rows, wide = rows_deep.shape[0], own_block.shape[0]
    cut = wide // 2

    def body(x_ref, a_ref, b_ref, o_ref, held, sems):
        copies = []
        for part in range(4):
            block, first = (a_ref, b_ref)[part // 2], (part % 2) * cut
            piece = block[first : first + cut, :] if by_rows else block[:, first : first + cut]
            held[part] = product(x_ref[:, :wide], piece).astype(bf16)
            copies.append(
                pltpu.make_async_copy(held.at[part], o_ref.at[:, pl.ds(part * cut, cut)], sems.at[part])
            )
            copies[-1].start()
        for copy in copies:
            copy.wait()

    size = 2 * (rows_deep.size + 2 * own_block.size + 2 * rows * wide)
    return pl.pallas_call(
        body,
        out_shape=pltpu.HBM((rows, 2 * wide), bf16),
        in_specs=[pl.BlockSpec(memory_space=pltpu.VMEM)] * 3,
        out_specs=pl.BlockSpec(memory_space=pltpu.HBM),
        scratch_shapes=[pltpu.VMEM((4, rows, cut), bf16), pltpu.SemaphoreType.DMA((4,))],
        cost_estimate=pl.CostEstimate(flops=4 * rows * wide * wide, bytes_accessed=size, transcendentals=0),
        compiler_params=pltpu.CompilerParams(vmem_limit_bytes=24 * 2**20),
    )(rows_deep, own_block, other_block)


def widen_near(product, rows_deep, own_block, other_block):
    rows, wide = rows_deep.shape[0], own_block.shape[0]

    def body(x_ref, a_ref, b_ref, o_ref):
        o_ref[:, :wide] = product(x_ref[:, :wide], a_ref[...]).astype(bf16)
        o_ref[:, wide:] = product(x_ref[:, :wide], b_ref[...]).astype(bf16)

    return call(
        body, [((rows, 2 * wide), bf16)], rows_deep, own_block, other_block, flops=4 * rows * wide * wide
    )


def narrow(product, rows_wide, own_block, other_block, beside=None):
    rows, wide = rows_wide.shape[0], rows_wide.shape[1] // 2
    more = [] if beside is None else [beside]

    def body(x_ref, a_ref, b_ref, *refs):
        total = product(x_ref[:, :wide], a_ref[...]) + product(x_ref[:, wide:], b_ref[...])
        refs[-1][:, :wide] = total.astype(bf16)
        if more:
            refs[-1][:, wide:] = refs[0][...]

    out = ((rows, wide * (1 + len(more))), bf16)
    return call(body, [out], rows_wide, own_block, other_block, *more, flops=4 * rows * wide * wide)


def add_up(ref, columns):
    total = ref[0, :, columns].astype(f32)
    for k in range(1, ref.shape[0]):
        total = total + ref[k, :, columns].astype(f32)
    return total


def strips(width, step):
    return [slice(first, first + step) for first in range(0, width, step)]


def sum_and_copy(landed, added):
    count, eight, wide = landed.shape

    def body(l_ref, a_ref, s_ref, c_ref):
        for cols in strips(wide, 128):
            total = a_ref[:, cols] + add_up(l_ref, cols)
            s_ref[:, cols] = total
            rounded = total.astype(bf16)
            for k in range(count):
                c_ref[k, :, cols] = rounded

    return call(body, [((eight, wide), f32), ((count, eight, wide), bf16)], landed, added)


def sum_half(landed, added, first):
    count, eight, wide = landed.shape
    half = wide // 2

    def body(l_ref, a_ref, o_ref):
        for cols in strips(half, 256):
            taken = slice(cols.start + first, cols.stop + first)
            o_ref[:, cols] = a_ref[:, taken] + add_up(l_ref, taken)

    return call(body, [((eight, half), f32)], landed, added)


def activate(landed):
    count, rows, deep = landed.shape

    def body(l_ref, p_ref, c_ref):
        for cols in strips(deep, 128):
            pre = add_up(l_ref, cols).astype(bf16)
            p_ref[:, cols] = pre
            value = gelu_parts(pre.astype(f32))[0].astype(bf16)
            for k in range(count):
                c_ref[k, :, cols] = value

    return call(body, [((rows, deep), bf16), ((count, rows, deep), bf16)], landed)


def activate_and_back(landed):
    count, rows, deep = landed.shape[0], landed.shape[1], landed.shape[2] // 2

    def body(l_ref, c_ref):
        for cols in strips(deep, 128):
            far = slice(cols.start + deep, cols.stop + deep)
            pre = add_up(l_ref, cols).astype(bf16)
            value, slope = gelu_parts(pre.astype(f32))
            value = value.astype(bf16)
            back = add_up(l_ref, far).astype(bf16)
            inner = (back.astype(f32) * slope).astype(bf16)
            for k in range(count):
                c_ref[k, :, cols] = inner
                c_ref[k, :, far] = value

    return call(body, [(landed.shape, bf16)], landed)


def back_through(landed, pre):
    count, rows, deep = landed.shape

    def body(l_ref, p_ref, c_ref):
        for cols in strips(deep, 128):
            slope = gelu_parts(p_ref[:, cols].astype(f32))[1]
            back = add_up(l_ref, cols).astype(bf16)
            inner = (back.astype(f32) * slope).astype(bf16)
            for k in range(count):
                c_ref[k, :, cols] = inner

    return call(body, [((count, rows, deep), bf16)], landed, pre)


def swap(block):
    return lax.ppermute(block, "core", [(0, 1), (1, 0)])


def swap_parts(block):
    step = block.shape[0] // 2
    return jnp.concatenate([swap(block[first : first + step]) for first in range(0, block.shape[0], step)], axis=0)


def exchange(parts, axes):
    return lax.all_to_all(parts, axes, 0, 0, tiled=True)


def shards(start_latent, target_one, target_two, w_up, w_down):
    n_y = SIZES["y"]
    n_h = SIZES["x"] * SIZES["z"]
    rows, wide = start_latent.shape
    deep = w_up.shape[1]
    eight = rows // (2 * n_h)
    half = rows // 2
    quarter = half // n_y
    core = lax.axis_index("core")
    place = lax.axis_index("x") * SIZES["z"] + lax.axis_index("z")

    def halves(full):
        cut = full.reshape(n_h, 2, eight, wide)
        own = lax.dynamic_index_in_dim(cut, core, 1, keepdims=False)
        other = lax.dynamic_index_in_dim(cut, 1 - core, 1, keepdims=False)
        return own, other

    def own_rows(*terms):
        first = 2 * eight * place
        pair = sum(lax.dynamic_slice_in_dim(full, first, 2 * eight, 0) for full in terms)
        mine = lax.dynamic_slice_in_dim(pair, eight * core, eight, 0)
        theirs = lax.dynamic_slice_in_dim(pair, eight * (1 - core), eight, 0)
        return jnp.concatenate([mine, swap(theirs)], axis=1)

    def rounded_halves(full):
        own, other = halves(full)
        return own.astype(bf16).reshape(half, wide), other.astype(bf16).reshape(half, wide)

    def both_cores(own, other_part):
        return (own + swap(other_part.astype(bf16)).astype(f32)).astype(bf16)

    down_other = swap(w_down)
    up_other = swap(w_up)

    start_own, start_other = rounded_halves(start_latent)
    pre_part = both_cores(dot(start_own, w_up), dot(start_other, w_up))
    pre_zero, act_zero = activate(exchange(pre_part.reshape(n_y, quarter, deep), "y"))
    act_zero, up_other = lax.optimization_barrier((exchange(act_zero, "y").reshape(half, deep), up_other))

    part = widen(dot, act_zero, w_down, down_other, False)
    landed = exchange(part.reshape(n_h, eight, 2 * wide), HIDDEN)
    two_own, two_other = rounded_halves(target_two)
    two_far = swap(two_other)
    start_far = swap(start_other)
    back_part = (dot_t(two_own, w_down) + dot_t(two_far, down_other)).astype(bf16)
    start_rows = own_rows(start_latent)
    target_rows = own_rows(target_one, target_two)
    landed, back_part, start_rows, target_rows, start_far = lax.optimization_barrier(
        (landed, back_part, start_rows, target_rows, start_far)
    )
    latent_one, input_one = sum_and_copy(landed, start_rows)
    input_one = exchange(input_one, HIDDEN).reshape(half, 2 * wide)

    both = narrow(dot, input_one, w_up, up_other, back_part).reshape(n_y, quarter, 2 * deep)
    one = activate_and_back(exchange(both, "y"))
    one = exchange(one, "y").reshape(half, 2 * deep)

    part = widen_near(dot_t, one, w_up, up_other)
    landed = exchange(part.reshape(n_h, eight, 2 * wide), HIDDEN)
    grad_one, error_one = sum_and_copy(landed, target_rows)
    error_one = exchange(error_one, HIDDEN).reshape(half, 2 * wide)

    back_part = narrow(dot_t, error_one, w_down, down_other)
    inner_zero = back_through(exchange(back_part.reshape(n_y, quarter, deep), "y"), pre_zero)
    inner_zero = exchange(inner_zero, "y").reshape(half, deep)

    part = widen(dot_t, inner_zero, w_up, up_other, True)
    part, inner_zero, error_one, one, act_zero, input_one = lax.optimization_barrier(
        (part, inner_zero, error_one, one, act_zero, input_one)
    )
    landed = exchange(part.reshape(n_h, eight, 2 * wide), HIDDEN)

    inner_both = jnp.concatenate([inner_zero, one[:, :deep]], axis=0)
    act_both = jnp.concatenate([act_zero, one[:, deep:]], axis=0)
    up_far = t_dot(jnp.concatenate([start_far, input_one[:, wide:]], axis=0), inner_both).astype(bf16)
    down_far = t_dot(act_both, jnp.concatenate([error_one[:, wide:], two_far], axis=0)).astype(bf16)
    grad_up = t_dot(jnp.concatenate([start_own, input_one[:, :wide]], axis=0), inner_both) + swap_parts(up_far)
    grad_down = t_dot(act_both, jnp.concatenate([error_one[:, :wide], two_own], axis=0)) + swap_parts(down_far)
    landed, grad_up, grad_down = lax.optimization_barrier((landed, grad_up, grad_down))

    theirs = swap(sum_half(landed, grad_one, wide))
    mine = sum_half(landed, grad_one, 0)
    grad_start = jnp.where(
        core == 0, jnp.concatenate([mine, theirs], axis=0), jnp.concatenate([theirs, mine], axis=0)
    )
    return (grad_start, grad_up, grad_down)


def solution(mesh):
    fine = Mesh(mesh.devices.reshape(tuple(SIZES.values())), tuple(SIZES))
    width, hidden = ("y", "core"), HIDDEN
    return jax.shard_map(
        shards,
        mesh=fine,
        in_specs=(
            P(None, width),
            P(None, width),
            P(None, width),
            P(width, hidden),
            P(hidden, width),
        ),
        out_specs=(P(hidden, width), P(width, hidden), P(hidden, width)),
        check_vma=False,
    )
```
